256 devices in a mesh: order: 32 (over z, x_hi, core), slab: 8 (over x_lo, y).
Axes of the slice: x: 4 (x_hi: 2, x_lo: 2; x = x_hi * 2 + x_lo), y: 4, z: 8, core: 2. Of those that a mesh axis runs over, the one named last changes fastest.
Arguments:
- direct: float32 [32, 2, 1024, 1024], P('order', None, 'slab'), may hold values from -6 to 6
- adjoint: float32 [32, 2, 1024, 1024], P('order', None, 'slab'), may hold values from -6 to 6
- sound: float32 [1024, 1024], P('slab'), may hold values from 0.5 to 4
- transverse: float32 [1024, 1024], replicated, may hold values from -0.1875 to 0.1875
- burner_temp: float32 [32], replicated, may hold values from -4 to 4
- burner_gain: float32 [32], replicated, may hold values from -4 to 4
- flame_cells: int32 [4096], replicated, may hold values from 0 to 1048575
- flame_weight: float32 [4096], replicated, may hold values from 0.5 to 4
- offsets: int32 [4], replicated, may hold values from 1 to 31
Outputs:
- image: float32 [32, 2, 1024, 1024], P('order', None, 'slab')
- coupling: float32 [32, 2, 4], P('order')
The draws below stay inside these ranges and needn't reach their ends.
All inputs are finite; a program needn't handle non-finite values.
Results may differ from the reference program's by a relative error of at most 0.0003.
Values sent between devices are 32-bit elements; how exact they have to be, the bound alone decides.
A program may use at most 128 MiB of HBM per device.

```python
import math
import jax
import jax.numpy as jnp
from jax import lax

AZ = 1024
FLAMES = 4096
OFFS = 4
ORDERS = 32
AX = 1024


def place_ends(entries, stream_key, low, high):
    longest = entries.shape.index(max(entries.shape))
    spots = []
    for shift in (0, 1):
        where = [jax.random.randint(jax.random.fold_in(stream_key, axis), (), 0, length) for axis, length in enumerate(entries.shape)]
        where[longest] = (where[longest] + shift) % entries.shape[longest]
        spots.append(tuple(where))
    return entries.at[spots[0]].set(low).at[spots[1]].set(high)


def level_of(key, dims, shards, low, high):
    def one(dim, blocks):
        draws = jax.random.uniform(jax.random.fold_in(jax.random.fold_in(key, 6), dim), (blocks,), jnp.float32, low / len(shards), high / len(shards))
        return jnp.repeat(jnp.exp(draws), dims[dim] // blocks).reshape((-1,) + (1,) * (len(dims) - dim - 1))

    loudness = one(*shards[0])
    for cut in shards[1:]:
        loudness = loudness * one(*cut)
    return loudness


def gaussian(own_key, shape, spread, bound, shards=(), kind=jnp.bfloat16):
    gain = level_of(own_key, shape, shards, -0.22, 0.18) if shards else 1.0
    values = jax.random.normal(own_key, shape, jnp.float32) * spread * gain
    return jnp.minimum(jnp.maximum(values, -bound), bound).astype(kind)


def setup_inputs(seed: int = 0) -> dict:
    key_of = jax.random.split(jax.random.key(seed), 10)
    return {
        "direct": gaussian(key_of[0], (ORDERS, 2, AX, AZ), 1.0, 6.0, ((0, 32), (2, 8)), jnp.float32),
        "adjoint": gaussian(key_of[1], (ORDERS, 2, AX, AZ), 1.0, 6.0, ((0, 32), (2, 8)), jnp.float32),
        "sound": jnp.clip(jnp.exp(math.log(4.0) - 2.0794415 * jax.random.uniform(key_of[2], (AX, AZ), jnp.float32) ** level_of(key_of[2], (AX, AZ), ((0, 8),), -0.2, 0.2)), 0.5, 4.0),
        "transverse": gaussian(key_of[3], (AZ, AZ), AZ ** -0.5, 0.1875, (), jnp.float32),
        "burner_temp": gaussian(key_of[4], (ORDERS,), 1.0, 4.0, (), jnp.float32),
        "burner_gain": gaussian(key_of[5], (ORDERS,), 1.0, 4.0, (), jnp.float32),
        "flame_cells": place_ends(jax.random.randint(key_of[6], (FLAMES,), 0, AX * AZ), jax.random.fold_in(key_of[6], 1), 0, (AX * AZ) - 1).astype(jnp.int32),
        "flame_weight": jnp.clip(jnp.exp(jax.random.uniform(key_of[7], (FLAMES,), jnp.float32, math.log(0.5), math.log(4.0))), 0.5, 4.0),
        "offsets": place_ends(jax.random.randint(key_of[8], (OFFS,), 1, ORDERS), jax.random.fold_in(key_of[8], 1), 1, ORDERS - 1).astype(jnp.int32),
    }


def apply_padded(padded, sound_padded, angle_now, transverse):
    center = padded[:, 1:-1]
    middle = sound_padded[1:-1]
    axial = 0.5 * (middle + sound_padded[2:]) * (center - padded[:, 2:]) + 0.5 * (middle + sound_padded[:-2]) * (center - padded[:, :-2])
    across = jnp.einsum('cxz,zw->cxw', center, transverse, precision=lax.Precision.HIGHEST)
    seam_weight = 0.5 * (middle[:, -1] + middle[:, 0])
    cos_turn = jnp.cos(angle_now)
    sin_turn = jnp.sin(angle_now)
    first_re = center[0, :, 0]
    first_im = center[1, :, 0]
    last_re = center[0, :, -1]
    last_im = center[1, :, -1]
    ahead_re = cos_turn * first_re - sin_turn * first_im
    ahead_im = sin_turn * first_re + cos_turn * first_im
    behind_re = cos_turn * last_re + sin_turn * last_im
    behind_im = cos_turn * last_im - sin_turn * last_re
    last_add = jnp.stack([seam_weight * (last_re - ahead_re), seam_weight * (last_im - ahead_im)])
    first_add = jnp.stack([seam_weight * (first_re - behind_re), seam_weight * (first_im - behind_im)])
    result = axial + across
    result = result.at[:, :, -1].add(last_add)
    result = result.at[:, :, 0].add(first_add)
    return result

def fourier_pair(values, offsets, orders):
    burner = jnp.arange(orders, dtype=jnp.int32)
    turns = offsets[:, None] * burner[None, :] % orders
    angles = 2.0 * math.pi / orders * turns.astype(values.dtype)
    real_part = lax.optimization_barrier(jnp.sum(values[None, :] * jnp.cos(angles), axis=1)) / orders
    imag_part = -lax.optimization_barrier(jnp.sum(values[None, :] * jnp.sin(angles), axis=1)) / orders
    return (real_part, imag_part)

def reference(direct, adjoint, sound, transverse, burner_temp, burner_gain, flame_cells, flame_weight, offsets):
    orders = ORDERS
    flame_field = jnp.zeros((AX * AZ,), flame_weight.dtype).at[flame_cells].add(flame_weight).reshape(AX, AZ)
    temp_re, temp_im = fourier_pair(burner_temp, offsets, orders)
    gain_re, gain_im = fourier_pair(burner_gain, offsets, orders)
    sound_padded = jnp.pad(sound, ((1, 1), (0, 0)))
    order_ids = jnp.arange(orders, dtype=jnp.int32)

    def own_image(order_now):
        angle_now = 2.0 * math.pi / orders * order_now.astype(direct.dtype)
        padded = jnp.pad(direct[order_now], ((0, 0), (1, 1), (0, 0)))
        return apply_padded(padded, sound_padded, angle_now, transverse)
    base = lax.map(own_image, order_ids)
    scale = 1.0 / math.sqrt(AX * AZ)

    def collect(order_now):
        total = base[order_now]
        adj = adjoint[order_now]
        rows_re = []
        rows_im = []
        for which in range(OFFS):
            source = (order_now - offsets[which]) % orders
            helm = base[source]
            field = direct[source]
            term_re = temp_re[which] * helm[0] - temp_im[which] * helm[1] + flame_field * (gain_re[which] * field[0] - gain_im[which] * field[1])
            term_im = temp_re[which] * helm[1] + temp_im[which] * helm[0] + flame_field * (gain_re[which] * field[1] + gain_im[which] * field[0])
            total = total + jnp.stack([term_re, term_im])
            rows_re.append(jnp.sum(adj[0] * term_re + adj[1] * term_im) * scale)
            rows_im.append(jnp.sum(adj[0] * term_im - adj[1] * term_re) * scale)
        return (total, jnp.stack([jnp.stack(rows_re), jnp.stack(rows_im)]))
    image, coupling = lax.map(collect, order_ids)
    return (image, coupling)
```

```python
import functools
import math

import jax
import jax.numpy as jnp
from jax import lax
from jax.experimental import pallas as pl
from jax.experimental.pallas import tpu as pltpu
from jax.sharding import PartitionSpec as P

MESH = pl.DeviceIdType.MESH
EARLY = 10


def kernel(
    orders,
    slabs,
    scale,
    direct_ref,
    adjoint_ref,
    sound_hbm,
    transverse_hbm,
    temp_ref,
    gain_ref,
    cells_ref,
    weight_ref,
    offsets_ref,
    image_ref,
    coupling_ref,
    dstage,
    astage,
    istage,
    field,
    adj,
    arrived,
    base,
    flamed,
    field_hi,
    field_lo,
    tmat,
    tmat_hi,
    tmat_lo,
    sound_pad,
    halo_send,
    halo_recv,
    turn_cos,
    turn_sin,
    csend,
    cpart,
    cslab,
    local_sem,
    send_sem,
    recv_sem,
):
    me = lax.axis_index("order")
    slab = lax.axis_index("slab")
    layers, width = direct_ref.shape[1], direct_ref.shape[2]
    rows = layers // orders
    last = width - 128
    offs = offsets_ref.shape[0]
    f32, bf16 = jnp.float32, jnp.bfloat16

    def order_dev(which):
        return {"order": which}

    def peer(step):
        return lax.rem(me + step, orders)

    fetch_t = pltpu.make_async_copy(transverse_hbm, tmat, local_sem.at[0])
    fetch_t.start()
    fetch_c = pltpu.make_async_copy(
        sound_hbm, sound_pad.at[pl.ds(8, layers)], local_sem.at[1]
    )
    fetch_c.start()

    barrier = pltpu.get_barrier_semaphore()

    def greet_order(step, carry):
        pl.semaphore_signal(
            barrier, inc=1, device_id=order_dev(peer(step)), device_id_type=MESH
        )
        return carry

    def greet_slab(step, carry):
        pl.semaphore_signal(
            barrier,
            inc=1,
            device_id={"slab": lax.rem(slab + step, slabs)},
            device_id_type=MESH,
        )
        return carry

    has_above_slab = jnp.logical_and(me == 0, slab > 0)
    has_below_slab = jnp.logical_and(me == orders - 1, slab < slabs - 1)
    has_above = jnp.logical_or(me > 0, slab > 0)
    has_below = jnp.logical_or(me < orders - 1, slab < slabs - 1)
    above_dev = {
        "order": lax.rem(me + orders - 1, orders),
        "slab": lax.rem(slab + slabs - lax.div(orders - me, orders), slabs),
    }
    below_dev = {
        "order": lax.rem(me + 1, orders),
        "slab": lax.rem(slab + lax.div(me + 1, orders), slabs),
    }
    lax.fori_loop(1, orders, greet_order, 0)
    lax.fori_loop(1, slabs, greet_slab, 0)

    @pl.when(has_above_slab)
    def _():
        pl.semaphore_signal(barrier, inc=1, device_id=above_dev, device_id_type=MESH)

    @pl.when(has_below_slab)
    def _():
        pl.semaphore_signal(barrier, inc=1, device_id=below_dev, device_id_type=MESH)

    sub = lax.broadcasted_iota(jnp.int32, (8, 128), 0)
    lane = lax.broadcasted_iota(jnp.int32, (8, 128), 1)
    sub_w = lax.broadcasted_iota(jnp.int32, (8, width), 0)

    def pack(source, stage):
        def body(tile, carry):
            at = pl.multiple_of(tile * 8, 8)
            re = source[0, pl.ds(at, 8), :]
            im = source[1, pl.ds(at, 8), :]
            stage[2 * tile] = jnp.where(sub_w < 4, re, pltpu.roll(im, 4, 0))
            stage[2 * tile + 1] = jnp.where(sub_w < 4, pltpu.roll(re, 4, 0), im)
            return carry

        lax.fori_loop(0, layers // 8, body, 0)

    pack(direct_ref, dstage)

    extra = has_above_slab.astype(jnp.int32) + has_below_slab.astype(jnp.int32)
    pl.semaphore_wait(barrier, orders - 1 + slabs - 1 + extra)

    def scatter_copy(stage, into, sem, step):
        to = peer(step)
        return pltpu.make_async_remote_copy(
            src_ref=stage.at[to],
            dst_ref=into.at[me],
            send_sem=send_sem.at[sem],
            recv_sem=recv_sem.at[sem],
            device_id=order_dev(to),
            device_id_type=MESH,
        )

    def scatter(stage, into, sem, first, end):
        def body(step, carry):
            scatter_copy(stage, into, sem, step).start()
            return carry

        lax.fori_loop(first, end, body, 0)

    def wait_bytes(ref, sem):
        pltpu.make_async_copy(ref, ref, sem).wait()

    def others(ref):
        return ref.at[pl.ds(0, orders - 1)]

    scatter(dstage, field, 0, 1, orders)
    field[me] = dstage[me]

    fetch_c.wait()

    def sound_up():
        return pltpu.make_async_remote_copy(
            src_ref=sound_pad.at[pl.ds(8, 8)],
            dst_ref=sound_pad.at[pl.ds(8 + layers, 8)],
            send_sem=send_sem.at[3],
            recv_sem=recv_sem.at[3],
            device_id={"slab": lax.rem(slab + slabs - 1, slabs)},
            device_id_type=MESH,
        )

    def sound_down():
        return pltpu.make_async_remote_copy(
            src_ref=sound_pad.at[pl.ds(layers, 8)],
            dst_ref=sound_pad.at[pl.ds(0, 8)],
            send_sem=send_sem.at[4],
            recv_sem=recv_sem.at[4],
            device_id={"slab": lax.rem(slab + 1, slabs)},
            device_id_type=MESH,
        )

    @pl.when(slab > 0)
    def _():
        sound_up().start()

    @pl.when(slab < slabs - 1)
    def _():
        sound_down().start()

    pack(adjoint_ref, astage)
    scatter(astage, adj, 1, 1, EARLY)
    adj[me] = astage[me]

    bin_ids = lax.broadcasted_iota(jnp.int32, (1, temp_ref.shape[1]), 1)
    tau_re, tau_im, gain_re, gain_im = [], [], [], []
    for j in range(offs):
        turns = lax.rem(offsets_ref[j] * bin_ids, orders)
        angles = 2.0 * math.pi / orders * turns.astype(f32)
        cos, sin = jnp.cos(angles), jnp.sin(angles)
        tau_re.append(jnp.sum(temp_ref[...] * cos) * (1.0 / orders))
        tau_im.append(-jnp.sum(temp_ref[...] * sin) * (1.0 / orders))
        gain_re.append(jnp.sum(gain_ref[...] * cos) * (1.0 / orders))
        gain_im.append(-jnp.sum(gain_ref[...] * sin) * (1.0 / orders))

    def turn_table(source, carry):
        angle = jnp.full((8, 128), 2.0 * math.pi / orders, f32) * source.astype(f32)
        turn_cos[source] = jnp.cos(angle)
        turn_sin[source] = jnp.where(sub < 4, -1.0, 1.0) * jnp.sin(angle)
        return carry

    lax.fori_loop(0, orders, turn_table, 0)

    first_cell = (slab * layers + me * rows) * width
    flame_step = 512
    flames = cells_ref.shape[1]
    sub_f = lax.broadcasted_iota(jnp.int32, (8, flame_step), 0)
    sub_c = lax.broadcasted_iota(jnp.int32, (width, flame_step), 0)

    def place(step, total):
        at = pl.multiple_of(step * flame_step, flame_step)
        ids = cells_ref[:, pl.ds(at, flame_step)] - first_cell
        weights = weight_ref[:, pl.ds(at, flame_step)]
        row = ids >> (width.bit_length() - 1)
        column = ids & (width - 1)
        mine = row == (sub_f & (rows - 1))
        spread = jnp.where(mine, weights, 0.0)
        hi = spread.astype(bf16)
        rest = spread - hi.astype(f32)
        mid = rest.astype(bf16)
        low = (rest - mid.astype(f32)).astype(bf16)
        pick = jnp.where(sub_c == column, 1.0, 0.0).astype(bf16)
        left = jnp.concatenate([hi.astype(f32), mid.astype(f32), low.astype(f32)], axis=0)
        part = lax.dot_general(
            left.astype(bf16), pick, (((1,), (1,)), ((), ())), preferred_element_type=f32
        )
        return total + (part[0:8] + part[8:16] + part[16:24])

    flame = lax.fori_loop(
        0, flames // flame_step, place, jnp.zeros((8, width), f32)
    )

    fetch_t.wait()

    def halves(block, carry):
        at = pl.ds(pl.multiple_of(block * 32, 32), 32)
        value = tmat[at, :]
        hi = value.astype(bf16)
        tmat_hi[at, :] = hi
        tmat_lo[at, :] = (value - hi.astype(f32)).astype(bf16)
        return carry

    lax.fori_loop(0, width // 32, halves, 0)

    @pl.when(slab < slabs - 1)
    def _():
        sound_up().wait_recv()

    @pl.when(slab > 0)
    def _():
        sound_down().wait_recv()

    @pl.when(slab < slabs - 1)
    def _():
        sound_down().wait_send()

    @pl.when(slab > 0)
    def _():
        sound_up().wait_send()

    @pl.when(slab == slabs - 1)
    def _():
        sound_pad[pl.ds(8 + layers, 8)] = jnp.zeros((8, width), f32)

    @pl.when(slab == 0)
    def _():
        sound_pad[pl.ds(0, 8)] = jnp.zeros((8, width), f32)

    tile = lax.div(me, 2)
    odd = lax.rem(me, 2) == 1
    top = sound_pad[pl.ds(pl.multiple_of(tile * 8, 8), 8), :]
    middle = sound_pad[pl.ds(pl.multiple_of(tile * 8 + 8, 8), 8), :]
    bottom = sound_pad[pl.ds(pl.multiple_of(tile * 8 + 16, 8), 8), :]
    low_half = sub_w < 4
    top_turned = pltpu.roll(top, 4, 0)
    middle_turned = pltpu.roll(middle, 4, 0)
    bottom_turned = pltpu.roll(bottom, 4, 0)
    own4 = jnp.where(odd, jnp.where(low_half, middle_turned, middle), jnp.where(low_half, middle, middle_turned))
    before = jnp.where(odd, middle, pltpu.roll(top, 4, 0))
    after = jnp.where(odd, bottom, middle_turned)
    above_row = jnp.where(low_half, pltpu.roll(before, 5, 0), pltpu.roll(before, 1, 0))
    below_row = jnp.where(low_half, pltpu.roll(after, 3, 0), pltpu.roll(after, 7, 0))
    place_in = sub_w & 3
    sound_above = jnp.where(place_in == 0, above_row, pltpu.roll(own4, 1, 0))
    sound_below = jnp.where(place_in == 3, below_row, pltpu.roll(own4, 7, 0))
    coef_below = 0.5 * (own4 + sound_below)
    coef_above = 0.5 * (own4 + sound_above)
    seam_first = 0.5 * (own4[:, 0:128] + pltpu.roll(own4[:, last:], 1, 1))
    seam_last = 0.5 * (own4[:, last:] + pltpu.roll(own4[:, 0:128], 127, 1))
    is_first = lane == 0
    is_last = lane == 127
    sign = jnp.where(sub < 4, -1.0, 1.0)
    sign_w = jnp.where(sub_w < 4, -1.0, 1.0)

    wait_bytes(others(field), recv_sem.at[0])

    def edges(group, carry):
        low = jnp.zeros((8, width), f32)
        high = jnp.zeros((8, width), f32)
        for i in range(4):
            value = field[4 * group + i]
            low = jnp.where(sub_w == 2 * i, pltpu.roll(value, (2 * i) % 8, 0), low)
            low = jnp.where(sub_w == 2 * i + 1, pltpu.roll(value, (2 * i + 5) % 8, 0), low)
            high = jnp.where(sub_w == 2 * i, pltpu.roll(value, (2 * i + 5) % 8, 0), high)
            high = jnp.where(sub_w == 2 * i + 1, pltpu.roll(value, (2 * i + 2) % 8, 0), high)
        at = pl.ds(pl.multiple_of(group * 8, 8), 8)
        halo_send[0, at, :] = low
        halo_send[1, at, :] = high
        return carry

    lax.fori_loop(0, orders // 4, edges, 0)

    def halo_up():
        return pltpu.make_async_remote_copy(
            src_ref=halo_send.at[0],
            dst_ref=halo_recv.at[1],
            send_sem=send_sem.at[5],
            recv_sem=recv_sem.at[5],
            device_id=above_dev,
            device_id_type=MESH,
        )

    def halo_down():
        return pltpu.make_async_remote_copy(
            src_ref=halo_send.at[1],
            dst_ref=halo_recv.at[0],
            send_sem=send_sem.at[6],
            recv_sem=recv_sem.at[6],
            device_id=below_dev,
            device_id_type=MESH,
        )

    @pl.when(has_above)
    def _():
        halo_up().start()

    @pl.when(has_below)
    def _():
        halo_down().start()

    scatter(astage, adj, 1, EARLY, orders)

    def split(group, carry):
        value = field[pl.ds(4 * group, 4)].reshape(32, width)
        at = pl.ds(pl.multiple_of(group * 32, 32), 32)
        hi = value.astype(bf16)
        field_hi[at, :] = hi
        field_lo[at, :] = (value - hi.astype(f32)).astype(bf16)
        return carry

    lax.fori_loop(0, orders // 4, split, 0)

    def across(block, carry):
        at = pl.ds(pl.multiple_of(block * 256, 256), 256)
        dot = functools.partial(jnp.dot, preferred_element_type=f32)
        t_hi = tmat_hi[:, at]
        t_lo = tmat_lo[:, at]
        hi = field_hi[...]
        product = dot(hi, t_lo) + dot(field_lo[...], t_hi) + dot(hi, t_hi)
        base[:, :, at] = product.reshape(orders, 8, 256)
        return carry

    lax.fori_loop(0, width // 256, across, 0)

    @pl.when(has_below)
    def _():
        halo_up_recv = halo_up()
        halo_up_recv.wait_recv()

    @pl.when(has_above)
    def _():
        halo_down_recv = halo_down()
        halo_down_recv.wait_recv()

    @pl.when(jnp.logical_not(has_below))
    def _():
        halo_recv[1] = jnp.zeros((2 * orders, width), f32)

    @pl.when(jnp.logical_not(has_above))
    def _():
        halo_recv[0] = jnp.zeros((2 * orders, width), f32)

    def helm(group, carry):
        at = pl.ds(pl.multiple_of(group * 8, 8), 8)
        upper = halo_recv[0, at, :]
        lower = halo_recv[1, at, :]
        for i in range(4):
            source = 4 * group + i
            value = field[source]
            up = jnp.where(
                sub_w == 0, pltpu.roll(upper, (8 - 2 * i) % 8, 0), pltpu.roll(value, 1, 0)
            )
            up = jnp.where(sub_w == 4, pltpu.roll(upper, (11 - 2 * i) % 8, 0), up)
            down = jnp.where(
                sub_w == 3, pltpu.roll(lower, (11 - 2 * i) % 8, 0), pltpu.roll(value, 7, 0)
            )
            down = jnp.where(sub_w == 7, pltpu.roll(lower, (14 - 2 * i) % 8, 0), down)
            axial = coef_below * (value - down) + coef_above * (value - up)
            base[source] = base[source] + axial
            flamed[source] = flame * value
            cos, sin = turn_cos[source], turn_sin[source]
            head, tail = value[:, 0:128], value[:, last:]
            tail_here = pltpu.roll(tail, 1, 1)
            head_here = pltpu.roll(head, 127, 1)
            behind = cos * tail_here - sin * pltpu.roll(tail_here, 4, 0)
            ahead = cos * head_here + sin * pltpu.roll(head_here, 4, 0)
            base[source, :, 0:128] = base[source, :, 0:128] + jnp.where(
                is_first, seam_first * (head - behind), 0.0
            )
            base[source, :, last:] = base[source, :, last:] + jnp.where(
                is_last, seam_last * (tail - ahead), 0.0
            )
        return carry

    lax.fori_loop(0, orders // 4, helm, 0)

    def mixed(target):
        plain = base[target]
        turned = jnp.zeros((8, width), f32)
        for j in range(offs):
            source = lax.rem(target - offsets_ref[j] + orders, orders)
            helm_src = base[source]
            flame_src = flamed[source]
            plain = plain + (helm_src * tau_re[j] + flame_src * gain_re[j])
            turned = turned + (helm_src * tau_im[j] + flame_src * gain_im[j])
        return plain + sign_w * pltpu.roll(turned, 4, 0)

    def give(step, carry):
        target = peer(step)
        istage[target] = mixed(target)
        scatter_copy(istage, arrived, 2, step).start()
        return carry

    lax.fori_loop(1, orders, give, 0)
    arrived[me] = mixed(me)

    wait_bytes(others(adj), recv_sem.at[1])
    row8 = lax.broadcasted_iota(jnp.int32, (8, 128), 0)

    def fold(value):
        total = value[:, 0:128]
        for block in range(1, width // 128):
            total = total + value[:, block * 128 : block * 128 + 128]
        return total

    def couple(target, carry):
        mine = adj[target]
        mine_turned = sign_w * pltpu.roll(mine, 4, 0)
        table = jnp.zeros((8, 128), f32)
        for j in range(offs):
            source = lax.rem(target - offsets_ref[j] + orders, orders)
            helm_src = base[source]
            flame_src = flamed[source]
            same = fold(mine * helm_src)
            cross = fold(mine_turned * helm_src)
            flame_same = fold(mine * flame_src)
            flame_cross = fold(mine_turned * flame_src)
            part_re = (
                tau_re[j] * same - tau_im[j] * cross
                + gain_re[j] * flame_same - gain_im[j] * flame_cross
            )
            part_im = (
                tau_re[j] * cross + tau_im[j] * same
                + gain_re[j] * flame_cross + gain_im[j] * flame_same
            )
            table = jnp.where(row8 == j, jnp.sum(part_re, axis=0, keepdims=True), table)
            table = jnp.where(
                row8 == offs + j, jnp.sum(part_im, axis=0, keepdims=True), table
            )
        column = jnp.sum(table, axis=1, keepdims=True)
        csend[target] = jnp.sum(
            jnp.where(lane == row8, column, 0.0), axis=0, keepdims=True
        )
        return carry

    lax.fori_loop(0, orders, couple, 0)
    scatter(csend, cpart, 7, 1, orders)
    cpart[me] = csend[me]
    wait_bytes(others(cpart), recv_sem.at[7])
    total = cpart[0]
    for k in range(1, orders):
        total = total + cpart[k]
    cslab[slab] = total

    def slab_copy(step):
        return pltpu.make_async_remote_copy(
            src_ref=cslab.at[slab],
            dst_ref=cslab.at[slab],
            send_sem=send_sem.at[8],
            recv_sem=recv_sem.at[8],
            device_id={"slab": lax.rem(slab + step, slabs)},
            device_id_type=MESH,
        )

    def slab_start(step, carry):
        slab_copy(step).start()
        return carry

    lax.fori_loop(1, slabs, slab_start, 0)

    wait_bytes(others(arrived), recv_sem.at[2])

    def unpack(tile_id, carry):
        at = pl.ds(pl.multiple_of(tile_id * 8, 8), 8)
        even = arrived[2 * tile_id]
        odd_tile = arrived[2 * tile_id + 1]
        image_ref[0, at, :] = jnp.where(low_half, even, pltpu.roll(odd_tile, 4, 0))
        image_ref[1, at, :] = jnp.where(low_half, pltpu.roll(even, 4, 0), odd_tile)
        return carry

    lax.fori_loop(0, layers // 8, unpack, 0)

    wait_bytes(cslab.at[pl.ds(0, slabs - 1)], recv_sem.at[8])
    whole = cslab[0]
    for k in range(1, slabs):
        whole = whole + cslab[k]
    whole = whole * scale
    coupling_ref[0:1, :] = whole[:, 0:offs]
    coupling_ref[1:2, :] = whole[:, offs : 2 * offs]

    wait_bytes(others(dstage), send_sem.at[0])
    wait_bytes(others(astage), send_sem.at[1])
    wait_bytes(others(istage), send_sem.at[2])
    wait_bytes(others(csend), send_sem.at[7])
    wait_bytes(cslab.at[pl.ds(0, slabs - 1)], send_sem.at[8])

    @pl.when(has_above)
    def _():
        halo_up().wait_send()

    @pl.when(has_below)
    def _():
        halo_down().wait_send()


def solution(mesh):
    orders = mesh.shape["order"]
    slabs = mesh.shape["slab"]

    def local(
        direct, adjoint, sound, transverse, burner_temp, burner_gain, flame_cells, flame_weight, offsets
    ):
        layers, width = direct.shape[2], direct.shape[3]
        offs = offsets.shape[0]
        f32, bf16 = jnp.float32, jnp.bfloat16
        vmem = pl.BlockSpec(memory_space=pltpu.VMEM)
        anywhere = pl.BlockSpec(memory_space=pl.ANY)
        block = (orders, 8, width)
        image, coupling = pl.pallas_call(
            functools.partial(
                kernel, orders, slabs, 1.0 / math.sqrt(layers * slabs * width)
            ),
            out_shape=(
                jax.ShapeDtypeStruct((2, layers, width), f32),
                jax.ShapeDtypeStruct((2, offs), f32),
            ),
            in_specs=[vmem, vmem, anywhere, anywhere, vmem, vmem, vmem, vmem]
            + [pl.BlockSpec(memory_space=pltpu.SMEM)],
            out_specs=(vmem, vmem),
            scratch_shapes=[
                pltpu.VMEM(block, f32),
                pltpu.VMEM(block, f32),
                pltpu.VMEM(block, f32),
                pltpu.VMEM(block, f32),
                pltpu.VMEM(block, f32),
                pltpu.VMEM(block, f32),
                pltpu.VMEM(block, f32),
                pltpu.VMEM(block, f32),
                pltpu.VMEM((orders * 8, width), bf16),
                pltpu.VMEM((orders * 8, width), bf16),
                pltpu.VMEM((width, width), f32),
                pltpu.VMEM((width, width), bf16),
                pltpu.VMEM((width, width), bf16),
                pltpu.VMEM((layers + 16, width), f32),
                pltpu.VMEM((2, 2 * orders, width), f32),
                pltpu.VMEM((2, 2 * orders, width), f32),
                pltpu.VMEM((orders, 8, 128), f32),
                pltpu.VMEM((orders, 8, 128), f32),
                pltpu.VMEM((orders, 1, 128), f32),
                pltpu.VMEM((orders, 1, 128), f32),
                pltpu.VMEM((slabs, 1, 128), f32),
                pltpu.SemaphoreType.DMA((2,)),
                pltpu.SemaphoreType.DMA((9,)),
                pltpu.SemaphoreType.DMA((9,)),
            ],
            compiler_params=pltpu.CompilerParams(
                collective_id=0, has_side_effects=True, vmem_limit_bytes=48 * 2**20
            ),
        )(
            direct[0],
            adjoint[0],
            sound,
            transverse,
            burner_temp[None],
            burner_gain[None],
            flame_cells[None],
            flame_weight[None],
            offsets,
        )
        return image[None], coupling[None]

    in_specs = (
        P("order", None, "slab", None),
        P("order", None, "slab", None),
        P("slab", None),
        P(),
        P(),
        P(),
        P(),
        P(),
        P(),
    )
    out_specs = (P("order", None, "slab", None), P("order", None, None))
    return jax.shard_map(local, mesh=mesh, in_specs=in_specs, out_specs=out_specs, check_vma=False)
```

```python
import functools
import math

import jax
import jax.numpy as jnp
from jax import lax
from jax.experimental import pallas as pl
from jax.experimental.pallas import tpu as pltpu
from jax.sharding import PartitionSpec as P

MESH = pl.DeviceIdType.MESH
STRIDE = 11
EARLY = 20
FIRST = 24
SECOND = 30


def kernel(
    orders,
    slabs,
    scale,
    direct_hbm,
    adjoint_hbm,
    sound_hbm,
    transverse_hbm,
    temp_hbm,
    gain_hbm,
    cells_hbm,
    weight_hbm,
    offsets_hbm,
    arrived,
    coupling_hbm,
    direct_ref,
    adjoint_ref,
    temp_ref,
    gain_ref,
    cells_ref,
    weight_ref,
    offsets_ref,
    dstage,
    astage,
    istage,
    field,
    adj,
    base,
    flamed,
    field_hi,
    field_lo,
    tmat,
    tmat_hi,
    tmat_lo,
    sound_pad,
    halo_send,
    halo_recv,
    turn_cos,
    turn_sin,
    csend,
    cpart,
    cslab,
    sums_ref,
    local_sem,
    send_sem,
    recv_sem,
):
    me = lax.axis_index("order")
    slab = lax.axis_index("slab")
    layers, width = direct_ref.shape[1], direct_ref.shape[2]
    rows = layers // orders
    last = width - 128
    offs = offsets_ref.shape[0]
    f32, bf16 = jnp.float32, jnp.bfloat16

    def order_dev(which):
        return {"order": which}

    def peer(step):
        return lax.rem(me + lax.rem(step * STRIDE, orders), orders)

    def fetch(source, into, sem):
        copy = pltpu.make_async_copy(source, into, local_sem.at[sem])
        copy.start()
        return copy

    fetch_d = fetch(direct_hbm, direct_ref, 2)

    barrier = pltpu.get_barrier_semaphore()

    def greet_order(step, carry):
        pl.semaphore_signal(
            barrier, inc=1, device_id=order_dev(peer(step)), device_id_type=MESH
        )
        return carry

    def greet_slab(step, carry):
        pl.semaphore_signal(
            barrier,
            inc=1,
            device_id={"slab": lax.rem(slab + step, slabs)},
            device_id_type=MESH,
        )
        return carry

    has_above_slab = jnp.logical_and(me == 0, slab > 0)
    has_below_slab = jnp.logical_and(me == orders - 1, slab < slabs - 1)
    has_above = jnp.logical_or(me > 0, slab > 0)
    has_below = jnp.logical_or(me < orders - 1, slab < slabs - 1)
    above_dev = {
        "order": lax.rem(me + orders - 1, orders),
        "slab": lax.rem(slab + slabs - lax.div(orders - me, orders), slabs),
    }
    below_dev = {
        "order": lax.rem(me + 1, orders),
        "slab": lax.rem(slab + lax.div(me + 1, orders), slabs),
    }
    lax.fori_loop(1, orders, greet_order, 0)
    lax.fori_loop(1, slabs, greet_slab, 0)

    @pl.when(has_above_slab)
    def _():
        pl.semaphore_signal(barrier, inc=1, device_id=above_dev, device_id_type=MESH)

    @pl.when(has_below_slab)
    def _():
        pl.semaphore_signal(barrier, inc=1, device_id=below_dev, device_id_type=MESH)

    sub = lax.broadcasted_iota(jnp.int32, (8, 128), 0)
    lane = lax.broadcasted_iota(jnp.int32, (8, 128), 1)
    sub_w = lax.broadcasted_iota(jnp.int32, (8, width), 0)

    def pack(source, stage):
        def body(tile, carry):
            at = pl.multiple_of(tile * 8, 8)
            re = source[0, pl.ds(at, 8), :]
            im = source[1, pl.ds(at, 8), :]
            stage[2 * tile] = jnp.where(sub_w < 4, re, pltpu.roll(im, 4, 0))
            stage[2 * tile + 1] = jnp.where(sub_w < 4, pltpu.roll(re, 4, 0), im)
            return carry

        lax.fori_loop(0, layers // 8, body, 0)

    fetch_c = fetch(sound_hbm, sound_pad.at[pl.ds(8, layers)], 1)
    fetch_a = fetch(adjoint_hbm, adjoint_ref, 3)
    small = [
        fetch(offsets_hbm, offsets_ref, 4),
        fetch(temp_hbm, temp_ref, 5),
        fetch(gain_hbm, gain_ref, 6),
        fetch(cells_hbm, cells_ref, 7),
        fetch(weight_hbm, weight_ref, 8),
    ]
    fetch_t = fetch(transverse_hbm, tmat, 0)
    fetch_d.wait()
    pack(direct_ref, dstage)

    extra = has_above_slab.astype(jnp.int32) + has_below_slab.astype(jnp.int32)
    pl.semaphore_wait(barrier, orders - 1 + slabs - 1 + extra)

    def scatter_copy(stage, into, sem, step):
        to = peer(step)
        return pltpu.make_async_remote_copy(
            src_ref=stage.at[to],
            dst_ref=into.at[me],
            send_sem=send_sem.at[sem],
            recv_sem=recv_sem.at[sem],
            device_id=order_dev(to),
            device_id_type=MESH,
        )

    def scatter(stage, into, sem, first, end):
        def body(step, carry):
            scatter_copy(stage, into, sem, step).start()
            return carry

        lax.fori_loop(first, end, body, 0)

    def wait_bytes(ref, sem):
        pltpu.make_async_copy(ref, ref, sem).wait()

    def others(ref):
        return ref.at[pl.ds(0, orders - 1)]

    scatter(dstage, field, 0, 1, orders)
    field[me] = dstage[me]

    fetch_c.wait()

    def sound_up():
        return pltpu.make_async_remote_copy(
            src_ref=sound_pad.at[pl.ds(8, 8)],
            dst_ref=sound_pad.at[pl.ds(8 + layers, 8)],
            send_sem=send_sem.at[3],
            recv_sem=recv_sem.at[3],
            device_id={"slab": lax.rem(slab + slabs - 1, slabs)},
            device_id_type=MESH,
        )

    def sound_down():
        return pltpu.make_async_remote_copy(
            src_ref=sound_pad.at[pl.ds(layers, 8)],
            dst_ref=sound_pad.at[pl.ds(0, 8)],
            send_sem=send_sem.at[4],
            recv_sem=recv_sem.at[4],
            device_id={"slab": lax.rem(slab + 1, slabs)},
            device_id_type=MESH,
        )

    @pl.when(slab > 0)
    def _():
        sound_up().start()

    @pl.when(slab < slabs - 1)
    def _():
        sound_down().start()

    fetch_a.wait()
    pack(adjoint_ref, astage)
    scatter(astage, adj, 1, 1, EARLY)
    adj[me] = astage[me]

    for copy in small:
        copy.wait()
    bin_ids = lax.broadcasted_iota(jnp.int32, (1, temp_ref.shape[1]), 1)
    tau_re, tau_im, gain_re, gain_im = [], [], [], []
    for j in range(offs):
        turns = lax.rem(offsets_ref[j] * bin_ids, orders)
        angles = 2.0 * math.pi / orders * turns.astype(f32)
        cos, sin = jnp.cos(angles), jnp.sin(angles)
        tau_re.append(jnp.sum(temp_ref[...] * cos) * (1.0 / orders))
        tau_im.append(-jnp.sum(temp_ref[...] * sin) * (1.0 / orders))
        gain_re.append(jnp.sum(gain_ref[...] * cos) * (1.0 / orders))
        gain_im.append(-jnp.sum(gain_ref[...] * sin) * (1.0 / orders))

    def turn_table(source, carry):
        angle = jnp.full((8, 128), 2.0 * math.pi / orders, f32) * source.astype(f32)
        turn_cos[source] = jnp.cos(angle)
        turn_sin[source] = jnp.where(sub < 4, -1.0, 1.0) * jnp.sin(angle)
        return carry

    lax.fori_loop(0, orders, turn_table, 0)

    first_cell = (slab * layers + me * rows) * width
    flame_step = 512
    flames = cells_ref.shape[1]
    sub_f = lax.broadcasted_iota(jnp.int32, (8, flame_step), 0)
    sub_c = lax.broadcasted_iota(jnp.int32, (width, flame_step), 0)

    def place(step, total):
        at = pl.multiple_of(step * flame_step, flame_step)
        ids = cells_ref[:, pl.ds(at, flame_step)] - first_cell
        weights = weight_ref[:, pl.ds(at, flame_step)]
        row = ids >> (width.bit_length() - 1)
        column = ids & (width - 1)
        mine = row == (sub_f & (rows - 1))
        spread = jnp.where(mine, weights, 0.0)
        hi = spread.astype(bf16)
        rest = spread - hi.astype(f32)
        mid = rest.astype(bf16)
        low = (rest - mid.astype(f32)).astype(bf16)
        pick = jnp.where(sub_c == column, 1.0, 0.0).astype(bf16)
        left = jnp.concatenate([hi.astype(f32), mid.astype(f32), low.astype(f32)], axis=0)
        part = lax.dot_general(
            left.astype(bf16), pick, (((1,), (1,)), ((), ())), preferred_element_type=f32
        )
        return total + (part[0:8] + part[8:16] + part[16:24])

    flame = lax.fori_loop(
        0, flames // flame_step, place, jnp.zeros((8, width), f32)
    )

    fetch_t.wait()

    def halves(block, carry):
        at = pl.ds(pl.multiple_of(block * 32, 32), 32)
        value = tmat[at, :]
        hi = value.astype(bf16)
        tmat_hi[at, :] = hi
        tmat_lo[at, :] = (value - hi.astype(f32)).astype(bf16)
        return carry

    lax.fori_loop(0, width // 32, halves, 0)

    @pl.when(slab < slabs - 1)
    def _():
        sound_up().wait_recv()

    @pl.when(slab > 0)
    def _():
        sound_down().wait_recv()

    @pl.when(slab < slabs - 1)
    def _():
        sound_down().wait_send()

    @pl.when(slab > 0)
    def _():
        sound_up().wait_send()

    @pl.when(slab == slabs - 1)
    def _():
        sound_pad[pl.ds(8 + layers, 8)] = jnp.zeros((8, width), f32)

    @pl.when(slab == 0)
    def _():
        sound_pad[pl.ds(0, 8)] = jnp.zeros((8, width), f32)

    tile = lax.div(me, 2)
    odd = lax.rem(me, 2) == 1
    top = sound_pad[pl.ds(pl.multiple_of(tile * 8, 8), 8), :]
    middle = sound_pad[pl.ds(pl.multiple_of(tile * 8 + 8, 8), 8), :]
    bottom = sound_pad[pl.ds(pl.multiple_of(tile * 8 + 16, 8), 8), :]
    low_half = sub_w < 4
    top_turned = pltpu.roll(top, 4, 0)
    middle_turned = pltpu.roll(middle, 4, 0)
    bottom_turned = pltpu.roll(bottom, 4, 0)
    own4 = jnp.where(odd, jnp.where(low_half, middle_turned, middle), jnp.where(low_half, middle, middle_turned))
    before = jnp.where(odd, middle, pltpu.roll(top, 4, 0))
    after = jnp.where(odd, bottom, middle_turned)
    above_row = jnp.where(low_half, pltpu.roll(before, 5, 0), pltpu.roll(before, 1, 0))
    below_row = jnp.where(low_half, pltpu.roll(after, 3, 0), pltpu.roll(after, 7, 0))
    place_in = sub_w & 3
    sound_above = jnp.where(place_in == 0, above_row, pltpu.roll(own4, 1, 0))
    sound_below = jnp.where(place_in == 3, below_row, pltpu.roll(own4, 7, 0))
    coef_below = 0.5 * (own4 + sound_below)
    coef_above = 0.5 * (own4 + sound_above)
    seam_first = 0.5 * (own4[:, 0:128] + pltpu.roll(own4[:, last:], 1, 1))
    seam_last = 0.5 * (own4[:, last:] + pltpu.roll(own4[:, 0:128], 127, 1))
    is_first = lane == 0
    is_last = lane == 127
    sign = jnp.where(sub < 4, -1.0, 1.0)
    sign_w = jnp.where(sub_w < 4, -1.0, 1.0)

    wait_bytes(others(field), recv_sem.at[0])

    def edges(group, carry):
        low = jnp.zeros((8, width), f32)
        high = jnp.zeros((8, width), f32)
        for i in range(4):
            value = field[4 * group + i]
            low = jnp.where(sub_w == 2 * i, pltpu.roll(value, (2 * i) % 8, 0), low)
            low = jnp.where(sub_w == 2 * i + 1, pltpu.roll(value, (2 * i + 5) % 8, 0), low)
            high = jnp.where(sub_w == 2 * i, pltpu.roll(value, (2 * i + 5) % 8, 0), high)
            high = jnp.where(sub_w == 2 * i + 1, pltpu.roll(value, (2 * i + 2) % 8, 0), high)
        at = pl.ds(pl.multiple_of(group * 8, 8), 8)
        halo_send[0, at, :] = low
        halo_send[1, at, :] = high
        return carry

    lax.fori_loop(0, orders // 4, edges, 0)

    def halo_up():
        return pltpu.make_async_remote_copy(
            src_ref=halo_send.at[0],
            dst_ref=halo_recv.at[1],
            send_sem=send_sem.at[5],
            recv_sem=recv_sem.at[5],
            device_id=above_dev,
            device_id_type=MESH,
        )

    def halo_down():
        return pltpu.make_async_remote_copy(
            src_ref=halo_send.at[1],
            dst_ref=halo_recv.at[0],
            send_sem=send_sem.at[6],
            recv_sem=recv_sem.at[6],
            device_id=below_dev,
            device_id_type=MESH,
        )

    @pl.when(has_above)
    def _():
        halo_up().start()

    @pl.when(has_below)
    def _():
        halo_down().start()

    scatter(astage, adj, 1, EARLY, orders)

    def split(group, carry):
        value = field[pl.ds(4 * group, 4)].reshape(32, width)
        at = pl.ds(pl.multiple_of(group * 32, 32), 32)
        hi = value.astype(bf16)
        field_hi[at, :] = hi
        field_lo[at, :] = (value - hi.astype(f32)).astype(bf16)
        return carry

    lax.fori_loop(0, orders // 4, split, 0)

    def across(block, carry):
        at = pl.ds(pl.multiple_of(block * 256, 256), 256)
        dot = functools.partial(jnp.dot, preferred_element_type=f32)
        t_hi = tmat_hi[:, at]
        t_lo = tmat_lo[:, at]
        hi = field_hi[...]
        product = dot(hi, t_lo) + dot(field_lo[...], t_hi) + dot(hi, t_hi)
        base[:, :, at] = product.reshape(orders, 8, 256)
        return carry

    lax.fori_loop(0, width // 256, across, 0)

    @pl.when(has_below)
    def _():
        halo_up_recv = halo_up()
        halo_up_recv.wait_recv()

    @pl.when(has_above)
    def _():
        halo_down_recv = halo_down()
        halo_down_recv.wait_recv()

    @pl.when(jnp.logical_not(has_below))
    def _():
        halo_recv[1] = jnp.zeros((2 * orders, width), f32)

    @pl.when(jnp.logical_not(has_above))
    def _():
        halo_recv[0] = jnp.zeros((2 * orders, width), f32)

    def helm(group, carry):
        at = pl.ds(pl.multiple_of(group * 8, 8), 8)
        upper = halo_recv[0, at, :]
        lower = halo_recv[1, at, :]
        for i in range(4):
            source = 4 * group + i
            value = field[source]
            up = jnp.where(
                sub_w == 0, pltpu.roll(upper, (8 - 2 * i) % 8, 0), pltpu.roll(value, 1, 0)
            )
            up = jnp.where(sub_w == 4, pltpu.roll(upper, (11 - 2 * i) % 8, 0), up)
            down = jnp.where(
                sub_w == 3, pltpu.roll(lower, (11 - 2 * i) % 8, 0), pltpu.roll(value, 7, 0)
            )
            down = jnp.where(sub_w == 7, pltpu.roll(lower, (14 - 2 * i) % 8, 0), down)
            axial = coef_below * (value - down) + coef_above * (value - up)
            base[source] = base[source] + axial
            flamed[source] = flame * value
            cos, sin = turn_cos[source], turn_sin[source]
            head, tail = value[:, 0:128], value[:, last:]
            tail_here = pltpu.roll(tail, 1, 1)
            head_here = pltpu.roll(head, 127, 1)
            behind = cos * tail_here - sin * pltpu.roll(tail_here, 4, 0)
            ahead = cos * head_here + sin * pltpu.roll(head_here, 4, 0)
            base[source, :, 0:128] = base[source, :, 0:128] + jnp.where(
                is_first, seam_first * (head - behind), 0.0
            )
            base[source, :, last:] = base[source, :, last:] + jnp.where(
                is_last, seam_last * (tail - ahead), 0.0
            )
        return carry

    lax.fori_loop(0, orders // 4, helm, 0)

    def mixed(target):
        plain = base[target]
        turned = jnp.zeros((8, width), f32)
        for j in range(offs):
            source = lax.rem(target - offsets_ref[j] + orders, orders)
            helm_src = base[source]
            flame_src = flamed[source]
            plain = plain + (helm_src * tau_re[j] + flame_src * gain_re[j])
            turned = turned + (helm_src * tau_im[j] + flame_src * gain_im[j])
        return plain + sign_w * pltpu.roll(turned, 4, 0)

    def give(step, carry):
        target = peer(step)
        istage[target] = mixed(target)
        scatter_copy(istage, arrived, 2, step).start()
        return carry

    lax.fori_loop(1, FIRST, give, 0)

    wait_bytes(others(adj), recv_sem.at[1])
    row8 = lax.broadcasted_iota(jnp.int32, (8, 128), 0)

    def fold(value):
        total = value[:, 0:128]
        for block in range(1, width // 128):
            total = total + value[:, block * 128 : block * 128 + 128]
        return total

    def couple(target, carry):
        mine = adj[target]
        mine_turned = sign_w * pltpu.roll(mine, 4, 0)
        table = jnp.zeros((8, 128), f32)
        for j in range(offs):
            source = lax.rem(target - offsets_ref[j] + orders, orders)
            helm_src = base[source]
            flame_src = flamed[source]
            same = fold(mine * helm_src)
            cross = fold(mine_turned * helm_src)
            flame_same = fold(mine * flame_src)
            flame_cross = fold(mine_turned * flame_src)
            part_re = (
                tau_re[j] * same - tau_im[j] * cross
                + gain_re[j] * flame_same - gain_im[j] * flame_cross
            )
            part_im = (
                tau_re[j] * cross + tau_im[j] * same
                + gain_re[j] * flame_cross + gain_im[j] * flame_same
            )
            table = jnp.where(row8 == j, jnp.sum(part_re, axis=0, keepdims=True), table)
            table = jnp.where(
                row8 == offs + j, jnp.sum(part_im, axis=0, keepdims=True), table
            )
        column = jnp.sum(table, axis=1, keepdims=True)
        csend[target] = jnp.sum(
            jnp.where(lane == row8, column, 0.0), axis=0, keepdims=True
        )
        return carry

    lax.fori_loop(0, orders, couple, 0)
    scatter(csend, cpart, 7, 1, orders)
    cpart[me] = csend[me]
    lax.fori_loop(FIRST, SECOND, give, 0)
    wait_bytes(others(cpart), recv_sem.at[7])
    total = cpart[0]
    for k in range(1, orders):
        total = total + cpart[k]
    cslab[slab] = total

    def slab_copy(step):
        return pltpu.make_async_remote_copy(
            src_ref=cslab.at[slab],
            dst_ref=cslab.at[slab],
            send_sem=send_sem.at[8],
            recv_sem=recv_sem.at[8],
            device_id={"slab": lax.rem(slab + step, slabs)},
            device_id_type=MESH,
        )

    def slab_start(step, carry):
        slab_copy(step).start()
        return carry

    lax.fori_loop(1, slabs, slab_start, 0)

    lax.fori_loop(SECOND, orders, give, 0)
    istage[me] = mixed(me)
    keep = pltpu.make_async_copy(istage.at[me], arrived.at[me], local_sem.at[9])
    keep.start()
    wait_bytes(cslab.at[pl.ds(0, slabs - 1)], recv_sem.at[8])
    whole = cslab[0]
    for k in range(1, slabs):
        whole = whole + cslab[k]
    whole = whole * scale
    sums_ref[0:1, :] = whole[:, 0:offs]
    sums_ref[1:2, :] = whole[:, offs : 2 * offs]
    give_sums = pltpu.make_async_copy(sums_ref, coupling_hbm, local_sem.at[10])
    give_sums.start()
    keep.wait()
    give_sums.wait()

    wait_bytes(others(arrived), recv_sem.at[2])
    wait_bytes(others(dstage), send_sem.at[0])
    wait_bytes(others(astage), send_sem.at[1])
    wait_bytes(others(istage), send_sem.at[2])
    wait_bytes(others(csend), send_sem.at[7])
    wait_bytes(cslab.at[pl.ds(0, slabs - 1)], send_sem.at[8])

    @pl.when(has_above)
    def _():
        halo_up().wait_send()

    @pl.when(has_below)
    def _():
        halo_down().wait_send()


def write_out(arrived_hbm, sums_hbm, image_hbm, coupling_hbm, arrived, image, sem):
    layers, width = image.shape[1], image.shape[2]
    low_half = lax.broadcasted_iota(jnp.int32, (8, width), 0) < 4
    pieces = 4
    part = layers // pieces
    blocks = arrived.shape[0] // pieces

    def pull(piece):
        at = pl.ds(piece * blocks, blocks)
        return pltpu.make_async_copy(arrived_hbm.at[at], arrived.at[at], sem.at[piece])

    def push(piece):
        at = pl.ds(piece * part, part)
        return pltpu.make_async_copy(
            image.at[:, at, :], image_hbm.at[:, at, :], sem.at[pieces + piece]
        )

    sums = pltpu.make_async_copy(sums_hbm, coupling_hbm, sem.at[2 * pieces])
    for piece in range(pieces):
        pull(piece).start()
    sums.start()
    for piece in range(pieces):
        pull(piece).wait()

        def unpack(step, carry):
            tile = piece * (part // 8) + step
            at = pl.ds(pl.multiple_of(tile * 8, 8), 8)
            even = arrived[2 * tile]
            odd = arrived[2 * tile + 1]
            image[0, at, :] = jnp.where(low_half, even, pltpu.roll(odd, 4, 0))
            image[1, at, :] = jnp.where(low_half, pltpu.roll(even, 4, 0), odd)
            return carry

        lax.fori_loop(0, part // 8, unpack, 0)
        push(piece).start()
    for piece in range(pieces):
        push(piece).wait()
    sums.wait()


def solution(mesh):
    orders = mesh.shape["order"]
    slabs = mesh.shape["slab"]

    def local(
        direct, adjoint, sound, transverse, burner_temp, burner_gain, flame_cells, flame_weight, offsets
    ):
        layers, width = direct.shape[2], direct.shape[3]
        offs = offsets.shape[0]
        f32, bf16 = jnp.float32, jnp.bfloat16
        hbm = pl.BlockSpec(memory_space=pltpu.HBM)
        block = (orders, 8, width)
        arrived, sums = pl.pallas_call(
            functools.partial(
                kernel, orders, slabs, 1.0 / math.sqrt(layers * slabs * width)
            ),
            out_shape=(
                jax.ShapeDtypeStruct(block, f32),
                jax.ShapeDtypeStruct((2, offs), f32),
            ),
            in_specs=[hbm] * 9,
            out_specs=(hbm, hbm),
            scratch_shapes=[
                pltpu.VMEM((2, layers, width), f32),
                pltpu.VMEM((2, layers, width), f32),
                pltpu.VMEM((1, burner_temp.shape[0]), f32),
                pltpu.VMEM((1, burner_gain.shape[0]), f32),
                pltpu.VMEM((1, flame_cells.shape[0]), jnp.int32),
                pltpu.VMEM((1, flame_weight.shape[0]), f32),
                pltpu.SMEM((offs,), jnp.int32),
                pltpu.VMEM(block, f32),
                pltpu.VMEM(block, f32),
                pltpu.VMEM(block, f32),
                pltpu.VMEM(block, f32),
                pltpu.VMEM(block, f32),
                pltpu.VMEM(block, f32),
                pltpu.VMEM(block, f32),
                pltpu.VMEM((orders * 8, width), bf16),
                pltpu.VMEM((orders * 8, width), bf16),
                pltpu.VMEM((width, width), f32),
                pltpu.VMEM((width, width), bf16),
                pltpu.VMEM((width, width), bf16),
                pltpu.VMEM((layers + 16, width), f32),
                pltpu.VMEM((2, 2 * orders, width), f32),
                pltpu.VMEM((2, 2 * orders, width), f32),
                pltpu.VMEM((orders, 8, 128), f32),
                pltpu.VMEM((orders, 8, 128), f32),
                pltpu.VMEM((orders, 1, 128), f32),
                pltpu.VMEM((orders, 1, 128), f32),
                pltpu.VMEM((slabs, 1, 128), f32),
                pltpu.VMEM((2, offs), f32),
                pltpu.SemaphoreType.DMA((11,)),
                pltpu.SemaphoreType.DMA((9,)),
                pltpu.SemaphoreType.DMA((9,)),
            ],
            compiler_params=pltpu.CompilerParams(
                collective_id=0, has_side_effects=True, vmem_limit_bytes=58 * 2**20
            ),
        )(
            direct[0],
            adjoint[0],
            sound,
            transverse,
            burner_temp[None],
            burner_gain[None],
            flame_cells[None],
            flame_weight[None],
            offsets,
        )
        image, coupling = pl.pallas_call(
            write_out,
            out_shape=(
                jax.ShapeDtypeStruct((2, layers, width), f32),
                jax.ShapeDtypeStruct((2, offs), f32),
            ),
            in_specs=[hbm, hbm],
            out_specs=(hbm, hbm),
            scratch_shapes=[
                pltpu.VMEM(block, f32),
                pltpu.VMEM((2, layers, width), f32),
                pltpu.SemaphoreType.DMA((9,)),
            ],
            compiler_params=pltpu.CompilerParams(vmem_limit_bytes=58 * 2**20),
        )(arrived, sums)
        return image[None], coupling[None]

    in_specs = (
        P("order", None, "slab", None),
        P("order", None, "slab", None),
        P("slab", None),
        P(),
        P(),
        P(),
        P(),
        P(),
        P(),
    )
    out_specs = (P("order", None, "slab", None), P("order", None, None))
    return jax.shard_map(local, mesh=mesh, in_specs=in_specs, out_specs=out_specs, check_vma=False)
```

```python
import functools
import math

import jax
import jax.numpy as jnp
from jax import lax
from jax.experimental import pallas as pl
from jax.experimental.pallas import tpu as pltpu
from jax.sharding import PartitionSpec as P

MESH = pl.DeviceIdType.MESH
STRIDE = 11
EARLY = 20
MIDDLE = 26
FIRST = 20


def kernel(
    orders,
    slabs,
    scale,
    direct_hbm,
    adjoint_hbm,
    sound_hbm,
    transverse_hbm,
    temp_hbm,
    gain_hbm,
    cells_hbm,
    weight_hbm,
    offsets_hbm,
    arrived,
    coupling_hbm,
    direct_ref,
    adjoint_ref,
    temp_ref,
    gain_ref,
    cells_ref,
    weight_ref,
    offsets_ref,
    dstage,
    astage,
    istage,
    field,
    adj,
    base,
    flamed,
    field_hi,
    field_lo,
    tmat,
    tmat_hi,
    tmat_lo,
    sound_pad,
    halo_send,
    halo_recv,
    halo_relay,
    turn_cos,
    turn_sin,
    csend,
    cpart,
    cslab,
    sums_ref,
    local_sem,
    send_sem,
    recv_sem,
):
    me = lax.axis_index("order")
    slab = lax.axis_index("slab")
    layers, width = direct_ref.shape[1], direct_ref.shape[2]
    rows = layers // orders
    last = width - 128
    offs = offsets_ref.shape[0]
    f32, bf16 = jnp.float32, jnp.bfloat16

    def order_dev(which):
        return {"order": which}

    def peer(step):
        return lax.rem(me + lax.rem(step * STRIDE, orders), orders)

    def fetch(source, into, sem):
        copy = pltpu.make_async_copy(source, into, local_sem.at[sem])
        copy.start()
        return copy

    fetch_d = fetch(direct_hbm, direct_ref, 2)

    barrier = pltpu.get_barrier_semaphore()

    def greet_order(step, carry):
        pl.semaphore_signal(
            barrier, inc=1, device_id=order_dev(peer(step)), device_id_type=MESH
        )
        return carry

    def greet_slab(step, carry):
        pl.semaphore_signal(
            barrier,
            inc=1,
            device_id={"slab": lax.rem(slab + step, slabs)},
            device_id_type=MESH,
        )
        return carry

    has_above_slab = jnp.logical_and(me == 0, slab > 0)
    has_below_slab = jnp.logical_and(me == orders - 1, slab < slabs - 1)
    has_above = jnp.logical_or(me > 0, slab > 0)
    has_below = jnp.logical_or(me < orders - 1, slab < slabs - 1)
    above_dev = {
        "order": lax.rem(me + orders - 1, orders),
        "slab": lax.rem(slab + slabs - lax.div(orders - me, orders), slabs),
    }
    below_dev = {
        "order": lax.rem(me + 1, orders),
        "slab": lax.rem(slab + lax.div(me + 1, orders), slabs),
    }
    place_in_plane = lax.rem(me, 4)
    crosses_up = jnp.logical_and(place_in_plane == 0, has_above)
    crosses_down = jnp.logical_and(place_in_plane == 3, has_below)
    within_up = jnp.logical_and(place_in_plane != 0, has_above)
    within_down = jnp.logical_and(place_in_plane != 3, has_below)
    relays_up = jnp.logical_and(
        place_in_plane == 2, jnp.logical_or(me > 3, slab > 0)
    )
    relays_down = jnp.logical_and(
        place_in_plane == 1, jnp.logical_or(me < orders - 4, slab < slabs - 1)
    )
    far_up_dev = {
        "order": lax.rem(me + orders - 3, orders),
        "slab": lax.rem(slab + slabs - lax.div(orders + 2 - me, orders), slabs),
    }
    far_down_dev = {
        "order": lax.rem(me + 3, orders),
        "slab": lax.rem(slab + lax.div(me + 3, orders), slabs),
    }
    greet_up_dev = {"order": orders - 3, "slab": lax.rem(slab + slabs - 1, slabs)}
    greet_down_dev = {"order": 2, "slab": lax.rem(slab + 1, slabs)}
    lax.fori_loop(1, orders, greet_order, 0)
    lax.fori_loop(1, slabs, greet_slab, 0)

    @pl.when(has_above_slab)
    def _():
        pl.semaphore_signal(barrier, inc=1, device_id=above_dev, device_id_type=MESH)
        pl.semaphore_signal(
            barrier, inc=1, device_id=greet_up_dev, device_id_type=MESH
        )

    @pl.when(has_below_slab)
    def _():
        pl.semaphore_signal(barrier, inc=1, device_id=below_dev, device_id_type=MESH)
        pl.semaphore_signal(
            barrier, inc=1, device_id=greet_down_dev, device_id_type=MESH
        )

    sub = lax.broadcasted_iota(jnp.int32, (8, 128), 0)
    lane = lax.broadcasted_iota(jnp.int32, (8, 128), 1)
    sub_w = lax.broadcasted_iota(jnp.int32, (8, width), 0)

    def pack(source, stage):
        def body(tile, carry):
            at = pl.multiple_of(tile * 8, 8)
            re = source[0, pl.ds(at, 8), :]
            im = source[1, pl.ds(at, 8), :]
            stage[2 * tile] = jnp.where(sub_w < 4, re, pltpu.roll(im, 4, 0))
            stage[2 * tile + 1] = jnp.where(sub_w < 4, pltpu.roll(re, 4, 0), im)
            return carry

        lax.fori_loop(0, layers // 8, body, 0)

    fetch_c = fetch(sound_hbm, sound_pad.at[pl.ds(8, layers)], 1)
    fetch_a = fetch(adjoint_hbm, adjoint_ref, 3)
    small = [
        fetch(offsets_hbm, offsets_ref, 4),
        fetch(temp_hbm, temp_ref, 5),
        fetch(gain_hbm, gain_ref, 6),
        fetch(cells_hbm, cells_ref, 7),
        fetch(weight_hbm, weight_ref, 8),
    ]
    fetch_t = fetch(transverse_hbm, tmat, 0)
    fetch_d.wait()
    pack(direct_ref, dstage)

    near_top = jnp.logical_and(me == 2, slab > 0)
    near_bottom = jnp.logical_and(me == orders - 3, slab < slabs - 1)
    extra = has_above_slab.astype(jnp.int32) + has_below_slab.astype(jnp.int32)
    extra = extra + near_top.astype(jnp.int32) + near_bottom.astype(jnp.int32)
    pl.semaphore_wait(barrier, orders - 1 + slabs - 1 + extra)

    def scatter_copy(stage, into, sem, step):
        to = peer(step)
        return pltpu.make_async_remote_copy(
            src_ref=stage.at[to],
            dst_ref=into.at[me],
            send_sem=send_sem.at[sem],
            recv_sem=recv_sem.at[sem],
            device_id=order_dev(to),
            device_id_type=MESH,
        )

    def scatter(stage, into, sem, first, end):
        def body(step, carry):
            scatter_copy(stage, into, sem, step).start()
            return carry

        lax.fori_loop(first, end, body, 0)

    def wait_bytes(ref, sem):
        pltpu.make_async_copy(ref, ref, sem).wait()

    def others(ref):
        return ref.at[pl.ds(0, orders - 1)]

    scatter(dstage, field, 0, 1, orders)
    field[me] = dstage[me]

    fetch_c.wait()

    def sound_up():
        return pltpu.make_async_remote_copy(
            src_ref=sound_pad.at[pl.ds(8, 8)],
            dst_ref=sound_pad.at[pl.ds(8 + layers, 8)],
            send_sem=send_sem.at[3],
            recv_sem=recv_sem.at[3],
            device_id={"slab": lax.rem(slab + slabs - 1, slabs)},
            device_id_type=MESH,
        )

    def sound_down():
        return pltpu.make_async_remote_copy(
            src_ref=sound_pad.at[pl.ds(layers, 8)],
            dst_ref=sound_pad.at[pl.ds(0, 8)],
            send_sem=send_sem.at[4],
            recv_sem=recv_sem.at[4],
            device_id={"slab": lax.rem(slab + 1, slabs)},
            device_id_type=MESH,
        )

    @pl.when(slab > 0)
    def _():
        sound_up().start()

    @pl.when(slab < slabs - 1)
    def _():
        sound_down().start()

    fetch_a.wait()
    pack(adjoint_ref, astage)
    scatter(astage, adj, 1, 1, EARLY)
    adj[me] = astage[me]

    for copy in small:
        copy.wait()
    bin_ids = lax.broadcasted_iota(jnp.int32, (1, temp_ref.shape[1]), 1)
    tau_re, tau_im, gain_re, gain_im = [], [], [], []
    for j in range(offs):
        turns = lax.rem(offsets_ref[j] * bin_ids, orders)
        angles = 2.0 * math.pi / orders * turns.astype(f32)
        cos, sin = jnp.cos(angles), jnp.sin(angles)
        tau_re.append(jnp.sum(temp_ref[...] * cos) * (1.0 / orders))
        tau_im.append(-jnp.sum(temp_ref[...] * sin) * (1.0 / orders))
        gain_re.append(jnp.sum(gain_ref[...] * cos) * (1.0 / orders))
        gain_im.append(-jnp.sum(gain_ref[...] * sin) * (1.0 / orders))

    def turn_table(source, carry):
        angle = jnp.full((8, 128), 2.0 * math.pi / orders, f32) * source.astype(f32)
        turn_cos[source] = jnp.cos(angle)
        turn_sin[source] = jnp.where(sub < 4, -1.0, 1.0) * jnp.sin(angle)
        return carry

    lax.fori_loop(0, orders, turn_table, 0)

    first_cell = (slab * layers + me * rows) * width
    flame_step = 512
    flames = cells_ref.shape[1]
    sub_f = lax.broadcasted_iota(jnp.int32, (8, flame_step), 0)
    sub_c = lax.broadcasted_iota(jnp.int32, (width, flame_step), 0)

    def place(step, total):
        at = pl.multiple_of(step * flame_step, flame_step)
        ids = cells_ref[:, pl.ds(at, flame_step)] - first_cell
        weights = weight_ref[:, pl.ds(at, flame_step)]
        row = ids >> (width.bit_length() - 1)
        column = ids & (width - 1)
        mine = row == (sub_f & (rows - 1))
        spread = jnp.where(mine, weights, 0.0)
        hi = spread.astype(bf16)
        rest = spread - hi.astype(f32)
        mid = rest.astype(bf16)
        low = (rest - mid.astype(f32)).astype(bf16)
        pick = jnp.where(sub_c == column, 1.0, 0.0).astype(bf16)
        left = jnp.concatenate([hi.astype(f32), mid.astype(f32), low.astype(f32)], axis=0)
        part = lax.dot_general(
            left.astype(bf16), pick, (((1,), (1,)), ((), ())), preferred_element_type=f32
        )
        return total + (part[0:8] + part[8:16] + part[16:24])

    flame = lax.fori_loop(
        0, flames // flame_step, place, jnp.zeros((8, width), f32)
    )

    fetch_t.wait()

    def halves(block, carry):
        at = pl.ds(pl.multiple_of(block * 32, 32), 32)
        value = tmat[at, :]
        hi = value.astype(bf16)
        tmat_hi[at, :] = hi
        tmat_lo[at, :] = (value - hi.astype(f32)).astype(bf16)
        return carry

    lax.fori_loop(0, width // 32, halves, 0)

    @pl.when(slab < slabs - 1)
    def _():
        sound_up().wait_recv()

    @pl.when(slab > 0)
    def _():
        sound_down().wait_recv()

    @pl.when(slab < slabs - 1)
    def _():
        sound_down().wait_send()

    @pl.when(slab > 0)
    def _():
        sound_up().wait_send()

    @pl.when(slab == slabs - 1)
    def _():
        sound_pad[pl.ds(8 + layers, 8)] = jnp.zeros((8, width), f32)

    @pl.when(slab == 0)
    def _():
        sound_pad[pl.ds(0, 8)] = jnp.zeros((8, width), f32)

    tile = lax.div(me, 2)
    odd = lax.rem(me, 2) == 1
    top = sound_pad[pl.ds(pl.multiple_of(tile * 8, 8), 8), :]
    middle = sound_pad[pl.ds(pl.multiple_of(tile * 8 + 8, 8), 8), :]
    bottom = sound_pad[pl.ds(pl.multiple_of(tile * 8 + 16, 8), 8), :]
    low_half = sub_w < 4
    top_turned = pltpu.roll(top, 4, 0)
    middle_turned = pltpu.roll(middle, 4, 0)
    bottom_turned = pltpu.roll(bottom, 4, 0)
    own4 = jnp.where(odd, jnp.where(low_half, middle_turned, middle), jnp.where(low_half, middle, middle_turned))
    before = jnp.where(odd, middle, pltpu.roll(top, 4, 0))
    after = jnp.where(odd, bottom, middle_turned)
    above_row = jnp.where(low_half, pltpu.roll(before, 5, 0), pltpu.roll(before, 1, 0))
    below_row = jnp.where(low_half, pltpu.roll(after, 3, 0), pltpu.roll(after, 7, 0))
    place_in = sub_w & 3
    sound_above = jnp.where(place_in == 0, above_row, pltpu.roll(own4, 1, 0))
    sound_below = jnp.where(place_in == 3, below_row, pltpu.roll(own4, 7, 0))
    coef_below = 0.5 * (own4 + sound_below)
    coef_above = 0.5 * (own4 + sound_above)
    seam_first = 0.5 * (own4[:, 0:128] + pltpu.roll(own4[:, last:], 1, 1))
    seam_last = 0.5 * (own4[:, last:] + pltpu.roll(own4[:, 0:128], 127, 1))
    is_first = lane == 0
    is_last = lane == 127
    sign = jnp.where(sub < 4, -1.0, 1.0)
    sign_w = jnp.where(sub_w < 4, -1.0, 1.0)

    wait_bytes(others(field), recv_sem.at[0])

    def edges(group, carry):
        low = jnp.zeros((8, width), f32)
        high = jnp.zeros((8, width), f32)
        for i in range(4):
            value = field[4 * group + i]
            low = jnp.where(sub_w == 2 * i, pltpu.roll(value, (2 * i) % 8, 0), low)
            low = jnp.where(sub_w == 2 * i + 1, pltpu.roll(value, (2 * i + 5) % 8, 0), low)
            high = jnp.where(sub_w == 2 * i, pltpu.roll(value, (2 * i + 5) % 8, 0), high)
            high = jnp.where(sub_w == 2 * i + 1, pltpu.roll(value, (2 * i + 2) % 8, 0), high)
        at = pl.ds(pl.multiple_of(group * 8, 8), 8)
        halo_send[0, at, :] = low
        halo_send[1, at, :] = high
        return carry

    lax.fori_loop(0, orders // 4, edges, 0)

    near, rest = pl.ds(0, orders), pl.ds(orders, orders)

    def halo(source, into, sem, recv, to):
        return pltpu.make_async_remote_copy(
            src_ref=source,
            dst_ref=into,
            send_sem=send_sem.at[sem],
            recv_sem=recv_sem.at[recv],
            device_id=to,
            device_id_type=MESH,
        )

    def up_near():
        return halo(halo_send.at[0, near], halo_recv.at[1, near], 5, 5, above_dev)

    def up_rest():
        return halo(halo_send.at[0, rest], halo_recv.at[1, rest], 9, 9, above_dev)

    def up_relay():
        return halo(halo_send.at[0, rest], halo_relay, 9, 11, order_dev(lax.rem(me + 2, orders)))

    def up_far():
        return halo(halo_relay, halo_recv.at[1, rest], 11, 9, far_up_dev)

    def down_near():
        return halo(halo_send.at[1, near], halo_recv.at[0, near], 6, 6, below_dev)

    def down_rest():
        return halo(halo_send.at[1, rest], halo_recv.at[0, rest], 10, 10, below_dev)

    def down_relay():
        return halo(halo_send.at[1, rest], halo_relay, 10, 11, order_dev(lax.rem(me + orders - 2, orders)))

    def down_far():
        return halo(halo_relay, halo_recv.at[0, rest], 11, 10, far_down_dev)

    @pl.when(crosses_up)
    def _():
        up_relay().start()

    @pl.when(crosses_down)
    def _():
        down_relay().start()

    @pl.when(has_above)
    def _():
        up_near().start()

    @pl.when(has_below)
    def _():
        down_near().start()

    @pl.when(within_up)
    def _():
        up_rest().start()

    @pl.when(within_down)
    def _():
        down_rest().start()

    scatter(astage, adj, 1, EARLY, MIDDLE)

    def split(group, carry):
        value = field[pl.ds(4 * group, 4)].reshape(32, width)
        at = pl.ds(pl.multiple_of(group * 32, 32), 32)
        hi = value.astype(bf16)
        field_hi[at, :] = hi
        field_lo[at, :] = (value - hi.astype(f32)).astype(bf16)
        return carry

    lax.fori_loop(0, orders // 4, split, 0)

    @pl.when(relays_up)
    def _():
        up_relay().wait_recv()
        up_far().start()

    @pl.when(relays_down)
    def _():
        down_relay().wait_recv()
        down_far().start()

    scatter(astage, adj, 1, MIDDLE, orders)

    def across(block, carry):
        at = pl.ds(pl.multiple_of(block * 256, 256), 256)
        dot = functools.partial(jnp.dot, preferred_element_type=f32)
        t_hi = tmat_hi[:, at]
        t_lo = tmat_lo[:, at]
        hi = field_hi[...]
        product = dot(hi, t_lo) + dot(field_lo[...], t_hi) + dot(hi, t_hi)
        base[:, :, at] = product.reshape(orders, 8, 256)
        return carry

    lax.fori_loop(0, width // 256, across, 0)

    @pl.when(has_below)
    def _():
        up_near().wait_recv()
        up_rest().wait_recv()

    @pl.when(has_above)
    def _():
        down_near().wait_recv()
        down_rest().wait_recv()

    @pl.when(jnp.logical_not(has_below))
    def _():
        halo_recv[1] = jnp.zeros((2 * orders, width), f32)

    @pl.when(jnp.logical_not(has_above))
    def _():
        halo_recv[0] = jnp.zeros((2 * orders, width), f32)

    def helm(group, carry):
        at = pl.ds(pl.multiple_of(group * 8, 8), 8)
        upper = halo_recv[0, at, :]
        lower = halo_recv[1, at, :]
        for i in range(4):
            source = 4 * group + i
            value = field[source]
            up = jnp.where(
                sub_w == 0, pltpu.roll(upper, (8 - 2 * i) % 8, 0), pltpu.roll(value, 1, 0)
            )
            up = jnp.where(sub_w == 4, pltpu.roll(upper, (11 - 2 * i) % 8, 0), up)
            down = jnp.where(
                sub_w == 3, pltpu.roll(lower, (11 - 2 * i) % 8, 0), pltpu.roll(value, 7, 0)
            )
            down = jnp.where(sub_w == 7, pltpu.roll(lower, (14 - 2 * i) % 8, 0), down)
            axial = coef_below * (value - down) + coef_above * (value - up)
            base[source] = base[source] + axial
            flamed[source] = flame * value
            cos, sin = turn_cos[source], turn_sin[source]
            head, tail = value[:, 0:128], value[:, last:]
            tail_here = pltpu.roll(tail, 1, 1)
            head_here = pltpu.roll(head, 127, 1)
            behind = cos * tail_here - sin * pltpu.roll(tail_here, 4, 0)
            ahead = cos * head_here + sin * pltpu.roll(head_here, 4, 0)
            base[source, :, 0:128] = base[source, :, 0:128] + jnp.where(
                is_first, seam_first * (head - behind), 0.0
            )
            base[source, :, last:] = base[source, :, last:] + jnp.where(
                is_last, seam_last * (tail - ahead), 0.0
            )
        return carry

    lax.fori_loop(0, orders // 4, helm, 0)

    def mixed(target):
        plain = base[target]
        turned = jnp.zeros((8, width), f32)
        for j in range(offs):
            source = lax.rem(target - offsets_ref[j] + orders, orders)
            helm_src = base[source]
            flame_src = flamed[source]
            plain = plain + (helm_src * tau_re[j] + flame_src * gain_re[j])
            turned = turned + (helm_src * tau_im[j] + flame_src * gain_im[j])
        return plain + sign_w * pltpu.roll(turned, 4, 0)

    def give(step, carry):
        target = peer(step)
        istage[target] = mixed(target)
        scatter_copy(istage, arrived, 2, step).start()
        return carry

    lax.fori_loop(1, FIRST, give, 0)

    wait_bytes(others(adj), recv_sem.at[1])
    row8 = lax.broadcasted_iota(jnp.int32, (8, 128), 0)

    def fold(value):
        total = value[:, 0:128]
        for block in range(1, width // 128):
            total = total + value[:, block * 128 : block * 128 + 128]
        return total

    def couple(target, carry):
        mine = adj[target]
        mine_turned = sign_w * pltpu.roll(mine, 4, 0)
        table = jnp.zeros((8, 128), f32)
        for j in range(offs):
            source = lax.rem(target - offsets_ref[j] + orders, orders)
            helm_src = base[source]
            flame_src = flamed[source]
            same = fold(mine * helm_src)
            cross = fold(mine_turned * helm_src)
            flame_same = fold(mine * flame_src)
            flame_cross = fold(mine_turned * flame_src)
            part_re = (
                tau_re[j] * same - tau_im[j] * cross
                + gain_re[j] * flame_same - gain_im[j] * flame_cross
            )
            part_im = (
                tau_re[j] * cross + tau_im[j] * same
                + gain_re[j] * flame_cross + gain_im[j] * flame_same
            )
            table = jnp.where(row8 == j, jnp.sum(part_re, axis=0, keepdims=True), table)
            table = jnp.where(
                row8 == offs + j, jnp.sum(part_im, axis=0, keepdims=True), table
            )
        column = jnp.sum(table, axis=1, keepdims=True)
        csend[target] = jnp.sum(
            jnp.where(lane == row8, column, 0.0), axis=0, keepdims=True
        )
        return carry

    lax.fori_loop(0, orders, couple, 0)
    scatter(csend, cpart, 7, 1, orders)
    cpart[me] = csend[me]
    lax.fori_loop(FIRST, orders, give, 0)
    wait_bytes(others(cpart), recv_sem.at[7])
    total = cpart[0]
    for k in range(1, orders):
        total = total + cpart[k]
    cslab[slab] = total

    def slab_copy(step):
        return pltpu.make_async_remote_copy(
            src_ref=cslab.at[slab],
            dst_ref=cslab.at[slab],
            send_sem=send_sem.at[8],
            recv_sem=recv_sem.at[8],
            device_id={"slab": lax.rem(slab + step, slabs)},
            device_id_type=MESH,
        )

    def slab_start(step, carry):
        slab_copy(step).start()
        return carry

    lax.fori_loop(1, slabs, slab_start, 0)

    istage[me] = mixed(me)
    keep = pltpu.make_async_copy(istage.at[me], arrived.at[me], local_sem.at[9])
    keep.start()
    wait_bytes(cslab.at[pl.ds(0, slabs - 1)], recv_sem.at[8])
    whole = cslab[0]
    for k in range(1, slabs):
        whole = whole + cslab[k]
    whole = whole * scale
    sums_ref[0:1, :] = whole[:, 0:offs]
    sums_ref[1:2, :] = whole[:, offs : 2 * offs]
    give_sums = pltpu.make_async_copy(sums_ref, coupling_hbm, local_sem.at[10])
    give_sums.start()
    keep.wait()
    give_sums.wait()

    wait_bytes(others(arrived), recv_sem.at[2])
    wait_bytes(others(dstage), send_sem.at[0])
    wait_bytes(others(astage), send_sem.at[1])
    wait_bytes(others(istage), send_sem.at[2])
    wait_bytes(others(csend), send_sem.at[7])
    wait_bytes(cslab.at[pl.ds(0, slabs - 1)], send_sem.at[8])

    @pl.when(has_above)
    def _():
        up_near().wait_send()
        up_rest().wait_send()

    @pl.when(has_below)
    def _():
        down_near().wait_send()
        down_rest().wait_send()

    @pl.when(relays_up)
    def _():
        up_far().wait_send()

    @pl.when(relays_down)
    def _():
        down_far().wait_send()


def write_out(arrived_hbm, sums_hbm, image_hbm, coupling_hbm, arrived, image, sem):
    layers, width = image.shape[1], image.shape[2]
    low_half = lax.broadcasted_iota(jnp.int32, (8, width), 0) < 4
    pieces = 4
    part = layers // pieces
    blocks = arrived.shape[0] // pieces

    def pull(piece):
        at = pl.ds(piece * blocks, blocks)
        return pltpu.make_async_copy(arrived_hbm.at[at], arrived.at[at], sem.at[piece])

    def push(piece):
        at = pl.ds(piece * part, part)
        return pltpu.make_async_copy(
            image.at[:, at, :], image_hbm.at[:, at, :], sem.at[pieces + piece]
        )

    sums = pltpu.make_async_copy(sums_hbm, coupling_hbm, sem.at[2 * pieces])
    for piece in range(pieces):
        pull(piece).start()
    sums.start()
    for piece in range(pieces):
        pull(piece).wait()

        def unpack(step, carry):
            tile = piece * (part // 8) + step
            at = pl.ds(pl.multiple_of(tile * 8, 8), 8)
            even = arrived[2 * tile]
            odd = arrived[2 * tile + 1]
            image[0, at, :] = jnp.where(low_half, even, pltpu.roll(odd, 4, 0))
            image[1, at, :] = jnp.where(low_half, pltpu.roll(even, 4, 0), odd)
            return carry

        lax.fori_loop(0, part // 8, unpack, 0)
        push(piece).start()
    for piece in range(pieces):
        push(piece).wait()
    sums.wait()


def solution(mesh):
    orders = mesh.shape["order"]
    slabs = mesh.shape["slab"]

    def local(
        direct, adjoint, sound, transverse, burner_temp, burner_gain, flame_cells, flame_weight, offsets
    ):
        layers, width = direct.shape[2], direct.shape[3]
        offs = offsets.shape[0]
        f32, bf16 = jnp.float32, jnp.bfloat16
        hbm = pl.BlockSpec(memory_space=pltpu.HBM)
        block = (orders, 8, width)
        arrived, sums = pl.pallas_call(
            functools.partial(
                kernel, orders, slabs, 1.0 / math.sqrt(layers * slabs * width)
            ),
            out_shape=(
                jax.ShapeDtypeStruct(block, f32),
                jax.ShapeDtypeStruct((2, offs), f32),
            ),
            in_specs=[hbm] * 9,
            out_specs=(hbm, hbm),
            scratch_shapes=[
                pltpu.VMEM((2, layers, width), f32),
                pltpu.VMEM((2, layers, width), f32),
                pltpu.VMEM((1, burner_temp.shape[0]), f32),
                pltpu.VMEM((1, burner_gain.shape[0]), f32),
                pltpu.VMEM((1, flame_cells.shape[0]), jnp.int32),
                pltpu.VMEM((1, flame_weight.shape[0]), f32),
                pltpu.SMEM((offs,), jnp.int32),
                pltpu.VMEM(block, f32),
                pltpu.VMEM(block, f32),
                pltpu.VMEM(block, f32),
                pltpu.VMEM(block, f32),
                pltpu.VMEM(block, f32),
                pltpu.VMEM(block, f32),
                pltpu.VMEM(block, f32),
                pltpu.VMEM((orders * 8, width), bf16),
                pltpu.VMEM((orders * 8, width), bf16),
                pltpu.VMEM((width, width), f32),
                pltpu.VMEM((width, width), bf16),
                pltpu.VMEM((width, width), bf16),
                pltpu.VMEM((layers + 16, width), f32),
                pltpu.VMEM((2, 2 * orders, width), f32),
                pltpu.VMEM((2, 2 * orders, width), f32),
                pltpu.VMEM((orders, width), f32),
                pltpu.VMEM((orders, 8, 128), f32),
                pltpu.VMEM((orders, 8, 128), f32),
                pltpu.VMEM((orders, 1, 128), f32),
                pltpu.VMEM((orders, 1, 128), f32),
                pltpu.VMEM((slabs, 1, 128), f32),
                pltpu.VMEM((2, offs), f32),
                pltpu.SemaphoreType.DMA((11,)),
                pltpu.SemaphoreType.DMA((12,)),
                pltpu.SemaphoreType.DMA((12,)),
            ],
            compiler_params=pltpu.CompilerParams(
                collective_id=0, has_side_effects=True, vmem_limit_bytes=58 * 2**20
            ),
        )(
            direct[0],
            adjoint[0],
            sound,
            transverse,
            burner_temp[None],
            burner_gain[None],
            flame_cells[None],
            flame_weight[None],
            offsets,
        )
        image, coupling = pl.pallas_call(
            write_out,
            out_shape=(
                jax.ShapeDtypeStruct((2, layers, width), f32),
                jax.ShapeDtypeStruct((2, offs), f32),
            ),
            in_specs=[hbm, hbm],
            out_specs=(hbm, hbm),
            scratch_shapes=[
                pltpu.VMEM(block, f32),
                pltpu.VMEM((2, layers, width), f32),
                pltpu.SemaphoreType.DMA((9,)),
            ],
            compiler_params=pltpu.CompilerParams(vmem_limit_bytes=58 * 2**20),
        )(arrived, sums)
        return image[None], coupling[None]

    in_specs = (
        P("order", None, "slab", None),
        P("order", None, "slab", None),
        P("slab", None),
        P(),
        P(),
        P(),
        P(),
        P(),
        P(),
    )
    out_specs = (P("order", None, "slab", None), P("order", None, None))
    return jax.shard_map(local, mesh=mesh, in_specs=in_specs, out_specs=out_specs, check_vma=False)
```

```python
import functools
import math

import jax
import jax.numpy as jnp
from jax import lax
from jax.experimental import pallas as pl
from jax.experimental.pallas import tpu as pltpu
from jax.sharding import PartitionSpec as P

MESH = pl.DeviceIdType.MESH
STRIDE = 11
IMAGE_STRIDE = 5
EARLY = 20
MIDDLE = 26
FIRST = 18


def kernel(
    orders,
    slabs,
    scale,
    direct_hbm,
    adjoint_hbm,
    sound_hbm,
    transverse_hbm,
    temp_hbm,
    gain_hbm,
    cells_hbm,
    weight_hbm,
    offsets_hbm,
    arrived,
    coupling_hbm,
    direct_ref,
    adjoint_ref,
    temp_ref,
    gain_ref,
    cells_ref,
    weight_ref,
    offsets_ref,
    dstage,
    astage,
    istage,
    field,
    adj,
    base,
    flamed,
    field_hi,
    field_lo,
    tmat,
    tmat_hi,
    tmat_lo,
    sound_pad,
    halo_send,
    halo_recv,
    halo_relay,
    turn_cos,
    turn_sin,
    csend,
    cpart,
    cslab,
    sums_ref,
    local_sem,
    send_sem,
    recv_sem,
):
    me = lax.axis_index("order")
    slab = lax.axis_index("slab")
    layers, width = direct_ref.shape[1], direct_ref.shape[2]
    rows = layers // orders
    last = width - 128
    offs = offsets_ref.shape[0]
    f32, bf16 = jnp.float32, jnp.bfloat16

    def order_dev(which):
        return {"order": which}

    def peer(step, stride=STRIDE):
        return lax.rem(me + lax.rem(step * stride, orders), orders)

    def fetch(source, into, sem):
        copy = pltpu.make_async_copy(source, into, local_sem.at[sem])
        copy.start()
        return copy

    fetch_d = fetch(direct_hbm, direct_ref, 2)

    barrier = pltpu.get_barrier_semaphore()

    def greet_order(step, carry):
        pl.semaphore_signal(
            barrier, inc=1, device_id=order_dev(peer(step)), device_id_type=MESH
        )
        return carry

    def greet_slab(step, carry):
        pl.semaphore_signal(
            barrier,
            inc=1,
            device_id={"slab": lax.rem(slab + step, slabs)},
            device_id_type=MESH,
        )
        return carry

    has_above_slab = jnp.logical_and(me == 0, slab > 0)
    has_below_slab = jnp.logical_and(me == orders - 1, slab < slabs - 1)
    has_above = jnp.logical_or(me > 0, slab > 0)
    has_below = jnp.logical_or(me < orders - 1, slab < slabs - 1)
    above_dev = {
        "order": lax.rem(me + orders - 1, orders),
        "slab": lax.rem(slab + slabs - lax.div(orders - me, orders), slabs),
    }
    below_dev = {
        "order": lax.rem(me + 1, orders),
        "slab": lax.rem(slab + lax.div(me + 1, orders), slabs),
    }
    place_in_plane = lax.rem(me, 4)
    crosses_up = jnp.logical_and(place_in_plane == 0, has_above)
    crosses_down = jnp.logical_and(place_in_plane == 3, has_below)
    within_up = jnp.logical_and(place_in_plane != 0, has_above)
    within_down = jnp.logical_and(place_in_plane != 3, has_below)
    relays_up = jnp.logical_and(
        place_in_plane == 2, jnp.logical_or(me > 3, slab > 0)
    )
    relays_down = jnp.logical_and(
        place_in_plane == 1, jnp.logical_or(me < orders - 4, slab < slabs - 1)
    )
    far_up_dev = {
        "order": lax.rem(me + orders - 3, orders),
        "slab": lax.rem(slab + slabs - lax.div(orders + 2 - me, orders), slabs),
    }
    far_down_dev = {
        "order": lax.rem(me + 3, orders),
        "slab": lax.rem(slab + lax.div(me + 3, orders), slabs),
    }
    greet_up_dev = {"order": orders - 3, "slab": lax.rem(slab + slabs - 1, slabs)}
    greet_down_dev = {"order": 2, "slab": lax.rem(slab + 1, slabs)}
    lax.fori_loop(1, orders, greet_order, 0)
    lax.fori_loop(1, slabs, greet_slab, 0)

    @pl.when(has_above_slab)
    def _():
        pl.semaphore_signal(barrier, inc=1, device_id=above_dev, device_id_type=MESH)
        pl.semaphore_signal(
            barrier, inc=1, device_id=greet_up_dev, device_id_type=MESH
        )

    @pl.when(has_below_slab)
    def _():
        pl.semaphore_signal(barrier, inc=1, device_id=below_dev, device_id_type=MESH)
        pl.semaphore_signal(
            barrier, inc=1, device_id=greet_down_dev, device_id_type=MESH
        )

    sub = lax.broadcasted_iota(jnp.int32, (8, 128), 0)
    lane = lax.broadcasted_iota(jnp.int32, (8, 128), 1)
    sub_w = lax.broadcasted_iota(jnp.int32, (8, width), 0)

    def pack(source, stage):
        def body(tile, carry):
            at = pl.multiple_of(tile * 8, 8)
            re = source[0, pl.ds(at, 8), :]
            im = source[1, pl.ds(at, 8), :]
            stage[2 * tile] = jnp.where(sub_w < 4, re, pltpu.roll(im, 4, 0))
            stage[2 * tile + 1] = jnp.where(sub_w < 4, pltpu.roll(re, 4, 0), im)
            return carry

        lax.fori_loop(0, layers // 8, body, 0)

    fetch_c = fetch(sound_hbm, sound_pad.at[pl.ds(8, layers)], 1)
    fetch_a = fetch(adjoint_hbm, adjoint_ref, 3)
    small = [
        fetch(offsets_hbm, offsets_ref, 4),
        fetch(temp_hbm, temp_ref, 5),
        fetch(gain_hbm, gain_ref, 6),
        fetch(cells_hbm, cells_ref, 7),
        fetch(weight_hbm, weight_ref, 8),
    ]
    fetch_t = fetch(transverse_hbm, tmat, 0)
    fetch_d.wait()
    pack(direct_ref, dstage)

    near_top = jnp.logical_and(me == 2, slab > 0)
    near_bottom = jnp.logical_and(me == orders - 3, slab < slabs - 1)
    extra = has_above_slab.astype(jnp.int32) + has_below_slab.astype(jnp.int32)
    extra = extra + near_top.astype(jnp.int32) + near_bottom.astype(jnp.int32)
    pl.semaphore_wait(barrier, orders - 1 + slabs - 1 + extra)

    def scatter_copy(stage, into, sem, step):
        to = peer(step, STRIDE if sem < 2 else IMAGE_STRIDE)
        return pltpu.make_async_remote_copy(
            src_ref=stage.at[to],
            dst_ref=into.at[me],
            send_sem=send_sem.at[sem],
            recv_sem=recv_sem.at[sem],
            device_id=order_dev(to),
            device_id_type=MESH,
        )

    def scatter(stage, into, sem, first, end):
        def body(step, carry):
            scatter_copy(stage, into, sem, step).start()
            return carry

        lax.fori_loop(first, end, body, 0)

    def wait_bytes(ref, sem):
        pltpu.make_async_copy(ref, ref, sem).wait()

    def others(ref):
        return ref.at[pl.ds(0, orders - 1)]

    scatter(dstage, field, 0, 1, orders)
    field[me] = dstage[me]

    fetch_c.wait()

    def sound_up():
        return pltpu.make_async_remote_copy(
            src_ref=sound_pad.at[pl.ds(8, 8)],
            dst_ref=sound_pad.at[pl.ds(8 + layers, 8)],
            send_sem=send_sem.at[3],
            recv_sem=recv_sem.at[3],
            device_id={"slab": lax.rem(slab + slabs - 1, slabs)},
            device_id_type=MESH,
        )

    def sound_down():
        return pltpu.make_async_remote_copy(
            src_ref=sound_pad.at[pl.ds(layers, 8)],
            dst_ref=sound_pad.at[pl.ds(0, 8)],
            send_sem=send_sem.at[4],
            recv_sem=recv_sem.at[4],
            device_id={"slab": lax.rem(slab + 1, slabs)},
            device_id_type=MESH,
        )

    @pl.when(slab > 0)
    def _():
        sound_up().start()

    @pl.when(slab < slabs - 1)
    def _():
        sound_down().start()

    fetch_a.wait()
    pack(adjoint_ref, astage)
    scatter(astage, adj, 1, 1, EARLY)
    adj[me] = astage[me]

    for copy in small:
        copy.wait()
    bin_ids = lax.broadcasted_iota(jnp.int32, (1, temp_ref.shape[1]), 1)
    tau_re, tau_im, gain_re, gain_im = [], [], [], []
    for j in range(offs):
        turns = lax.rem(offsets_ref[j] * bin_ids, orders)
        angles = 2.0 * math.pi / orders * turns.astype(f32)
        cos, sin = jnp.cos(angles), jnp.sin(angles)
        tau_re.append(jnp.sum(temp_ref[...] * cos) * (1.0 / orders))
        tau_im.append(-jnp.sum(temp_ref[...] * sin) * (1.0 / orders))
        gain_re.append(jnp.sum(gain_ref[...] * cos) * (1.0 / orders))
        gain_im.append(-jnp.sum(gain_ref[...] * sin) * (1.0 / orders))

    def turn_table(source, carry):
        angle = jnp.full((8, 128), 2.0 * math.pi / orders, f32) * source.astype(f32)
        turn_cos[source] = jnp.cos(angle)
        turn_sin[source] = jnp.where(sub < 4, -1.0, 1.0) * jnp.sin(angle)
        return carry

    lax.fori_loop(0, orders, turn_table, 0)

    first_cell = (slab * layers + me * rows) * width
    flame_step = 512
    flames = cells_ref.shape[1]
    sub_f = lax.broadcasted_iota(jnp.int32, (8, flame_step), 0)
    sub_c = lax.broadcasted_iota(jnp.int32, (width, flame_step), 0)

    def place(step, total):
        at = pl.multiple_of(step * flame_step, flame_step)
        ids = cells_ref[:, pl.ds(at, flame_step)] - first_cell
        weights = weight_ref[:, pl.ds(at, flame_step)]
        row = ids >> (width.bit_length() - 1)
        column = ids & (width - 1)
        mine = row == (sub_f & (rows - 1))
        spread = jnp.where(mine, weights, 0.0)
        hi = spread.astype(bf16)
        rest = spread - hi.astype(f32)
        mid = rest.astype(bf16)
        low = (rest - mid.astype(f32)).astype(bf16)
        pick = jnp.where(sub_c == column, 1.0, 0.0).astype(bf16)
        left = jnp.concatenate([hi.astype(f32), mid.astype(f32), low.astype(f32)], axis=0)
        part = lax.dot_general(
            left.astype(bf16), pick, (((1,), (1,)), ((), ())), preferred_element_type=f32
        )
        return total + (part[0:8] + part[8:16] + part[16:24])

    flame = lax.fori_loop(
        0, flames // flame_step, place, jnp.zeros((8, width), f32)
    )

    fetch_t.wait()

    def halves(block, carry):
        at = pl.ds(pl.multiple_of(block * 32, 32), 32)
        value = tmat[at, :]
        hi = value.astype(bf16)
        tmat_hi[at, :] = hi
        tmat_lo[at, :] = (value - hi.astype(f32)).astype(bf16)
        return carry

    lax.fori_loop(0, width // 32, halves, 0)

    @pl.when(slab < slabs - 1)
    def _():
        sound_up().wait_recv()

    @pl.when(slab > 0)
    def _():
        sound_down().wait_recv()

    @pl.when(slab < slabs - 1)
    def _():
        sound_down().wait_send()

    @pl.when(slab > 0)
    def _():
        sound_up().wait_send()

    @pl.when(slab == slabs - 1)
    def _():
        sound_pad[pl.ds(8 + layers, 8)] = jnp.zeros((8, width), f32)

    @pl.when(slab == 0)
    def _():
        sound_pad[pl.ds(0, 8)] = jnp.zeros((8, width), f32)

    tile = lax.div(me, 2)
    odd = lax.rem(me, 2) == 1
    top = sound_pad[pl.ds(pl.multiple_of(tile * 8, 8), 8), :]
    middle = sound_pad[pl.ds(pl.multiple_of(tile * 8 + 8, 8), 8), :]
    bottom = sound_pad[pl.ds(pl.multiple_of(tile * 8 + 16, 8), 8), :]
    low_half = sub_w < 4
    top_turned = pltpu.roll(top, 4, 0)
    middle_turned = pltpu.roll(middle, 4, 0)
    bottom_turned = pltpu.roll(bottom, 4, 0)
    own4 = jnp.where(odd, jnp.where(low_half, middle_turned, middle), jnp.where(low_half, middle, middle_turned))
    before = jnp.where(odd, middle, pltpu.roll(top, 4, 0))
    after = jnp.where(odd, bottom, middle_turned)
    above_row = jnp.where(low_half, pltpu.roll(before, 5, 0), pltpu.roll(before, 1, 0))
    below_row = jnp.where(low_half, pltpu.roll(after, 3, 0), pltpu.roll(after, 7, 0))
    place_in = sub_w & 3
    sound_above = jnp.where(place_in == 0, above_row, pltpu.roll(own4, 1, 0))
    sound_below = jnp.where(place_in == 3, below_row, pltpu.roll(own4, 7, 0))
    coef_below = 0.5 * (own4 + sound_below)
    coef_above = 0.5 * (own4 + sound_above)
    seam_first = 0.5 * (own4[:, 0:128] + pltpu.roll(own4[:, last:], 1, 1))
    seam_last = 0.5 * (own4[:, last:] + pltpu.roll(own4[:, 0:128], 127, 1))
    is_first = lane == 0
    is_last = lane == 127
    sign = jnp.where(sub < 4, -1.0, 1.0)
    sign_w = jnp.where(sub_w < 4, -1.0, 1.0)

    wait_bytes(others(field), recv_sem.at[0])

    def edges(group, carry):
        low = jnp.zeros((8, width), f32)
        high = jnp.zeros((8, width), f32)
        for i in range(4):
            value = field[4 * group + i]
            low = jnp.where(sub_w == 2 * i, pltpu.roll(value, (2 * i) % 8, 0), low)
            low = jnp.where(sub_w == 2 * i + 1, pltpu.roll(value, (2 * i + 5) % 8, 0), low)
            high = jnp.where(sub_w == 2 * i, pltpu.roll(value, (2 * i + 5) % 8, 0), high)
            high = jnp.where(sub_w == 2 * i + 1, pltpu.roll(value, (2 * i + 2) % 8, 0), high)
        at = pl.ds(pl.multiple_of(group * 8, 8), 8)
        halo_send[0, at, :] = low
        halo_send[1, at, :] = high
        return carry

    lax.fori_loop(0, orders // 4, edges, 0)

    near, rest = pl.ds(0, orders), pl.ds(orders, orders)

    def halo(source, into, sem, recv, to):
        return pltpu.make_async_remote_copy(
            src_ref=source,
            dst_ref=into,
            send_sem=send_sem.at[sem],
            recv_sem=recv_sem.at[recv],
            device_id=to,
            device_id_type=MESH,
        )

    def up_near():
        return halo(halo_send.at[0, near], halo_recv.at[1, near], 5, 5, above_dev)

    def up_rest():
        return halo(halo_send.at[0, rest], halo_recv.at[1, rest], 9, 9, above_dev)

    def up_relay():
        return halo(halo_send.at[0, rest], halo_relay, 9, 11, order_dev(lax.rem(me + 2, orders)))

    def up_far():
        return halo(halo_relay, halo_recv.at[1, rest], 11, 9, far_up_dev)

    def down_near():
        return halo(halo_send.at[1, near], halo_recv.at[0, near], 6, 6, below_dev)

    def down_rest():
        return halo(halo_send.at[1, rest], halo_recv.at[0, rest], 10, 10, below_dev)

    def down_relay():
        return halo(halo_send.at[1, rest], halo_relay, 10, 11, order_dev(lax.rem(me + orders - 2, orders)))

    def down_far():
        return halo(halo_relay, halo_recv.at[0, rest], 11, 10, far_down_dev)

    @pl.when(crosses_up)
    def _():
        up_relay().start()

    @pl.when(crosses_down)
    def _():
        down_relay().start()

    @pl.when(has_above)
    def _():
        up_near().start()

    @pl.when(has_below)
    def _():
        down_near().start()

    @pl.when(within_up)
    def _():
        up_rest().start()

    @pl.when(within_down)
    def _():
        down_rest().start()

    scatter(astage, adj, 1, EARLY, MIDDLE)

    def split(group, carry):
        value = field[pl.ds(4 * group, 4)].reshape(32, width)
        at = pl.ds(pl.multiple_of(group * 32, 32), 32)
        hi = value.astype(bf16)
        field_hi[at, :] = hi
        field_lo[at, :] = (value - hi.astype(f32)).astype(bf16)
        return carry

    lax.fori_loop(0, orders // 4, split, 0)

    @pl.when(relays_up)
    def _():
        up_relay().wait_recv()
        up_far().start()

    @pl.when(relays_down)
    def _():
        down_relay().wait_recv()
        down_far().start()

    scatter(astage, adj, 1, MIDDLE, orders)

    def across(block, carry):
        at = pl.ds(pl.multiple_of(block * 256, 256), 256)
        dot = functools.partial(jnp.dot, preferred_element_type=f32)
        t_hi = tmat_hi[:, at]
        t_lo = tmat_lo[:, at]
        hi = field_hi[...]
        product = dot(hi, t_lo) + dot(field_lo[...], t_hi) + dot(hi, t_hi)
        base[:, :, at] = product.reshape(orders, 8, 256)
        return carry

    lax.fori_loop(0, width // 256, across, 0)

    @pl.when(has_below)
    def _():
        up_near().wait_recv()
        up_rest().wait_recv()

    @pl.when(has_above)
    def _():
        down_near().wait_recv()
        down_rest().wait_recv()

    @pl.when(jnp.logical_not(has_below))
    def _():
        halo_recv[1] = jnp.zeros((2 * orders, width), f32)

    @pl.when(jnp.logical_not(has_above))
    def _():
        halo_recv[0] = jnp.zeros((2 * orders, width), f32)

    def helm(group, carry):
        at = pl.ds(pl.multiple_of(group * 8, 8), 8)
        upper = halo_recv[0, at, :]
        lower = halo_recv[1, at, :]
        for i in range(4):
            source = 4 * group + i
            value = field[source]
            up = jnp.where(
                sub_w == 0, pltpu.roll(upper, (8 - 2 * i) % 8, 0), pltpu.roll(value, 1, 0)
            )
            up = jnp.where(sub_w == 4, pltpu.roll(upper, (11 - 2 * i) % 8, 0), up)
            down = jnp.where(
                sub_w == 3, pltpu.roll(lower, (11 - 2 * i) % 8, 0), pltpu.roll(value, 7, 0)
            )
            down = jnp.where(sub_w == 7, pltpu.roll(lower, (14 - 2 * i) % 8, 0), down)
            axial = coef_below * (value - down) + coef_above * (value - up)
            base[source] = base[source] + axial
            flamed[source] = flame * value
            cos, sin = turn_cos[source], turn_sin[source]
            head, tail = value[:, 0:128], value[:, last:]
            tail_here = pltpu.roll(tail, 1, 1)
            head_here = pltpu.roll(head, 127, 1)
            behind = cos * tail_here - sin * pltpu.roll(tail_here, 4, 0)
            ahead = cos * head_here + sin * pltpu.roll(head_here, 4, 0)
            base[source, :, 0:128] = base[source, :, 0:128] + jnp.where(
                is_first, seam_first * (head - behind), 0.0
            )
            base[source, :, last:] = base[source, :, last:] + jnp.where(
                is_last, seam_last * (tail - ahead), 0.0
            )
        return carry

    lax.fori_loop(0, orders // 4, helm, 0)

    def mixed(target):
        plain = base[target]
        turned = jnp.zeros((8, width), f32)
        for j in range(offs):
            source = lax.rem(target - offsets_ref[j] + orders, orders)
            helm_src = base[source]
            flame_src = flamed[source]
            plain = plain + (helm_src * tau_re[j] + flame_src * gain_re[j])
            turned = turned + (helm_src * tau_im[j] + flame_src * gain_im[j])
        return plain + sign_w * pltpu.roll(turned, 4, 0)

    def give(step, carry):
        target = peer(step, IMAGE_STRIDE)
        istage[target] = mixed(target)
        scatter_copy(istage, arrived, 2, step).start()
        return carry

    lax.fori_loop(1, FIRST, give, 0)

    wait_bytes(others(adj), recv_sem.at[1])
    row8 = lax.broadcasted_iota(jnp.int32, (8, 128), 0)

    def fold(value):
        total = value[:, 0:128]
        for block in range(1, width // 128):
            total = total + value[:, block * 128 : block * 128 + 128]
        return total

    def couple(target, carry):
        mine = adj[target]
        mine_turned = sign_w * pltpu.roll(mine, 4, 0)
        table = jnp.zeros((8, 128), f32)
        for j in range(offs):
            source = lax.rem(target - offsets_ref[j] + orders, orders)
            helm_src = base[source]
            flame_src = flamed[source]
            same = fold(mine * helm_src)
            cross = fold(mine_turned * helm_src)
            flame_same = fold(mine * flame_src)
            flame_cross = fold(mine_turned * flame_src)
            part_re = (
                tau_re[j] * same - tau_im[j] * cross
                + gain_re[j] * flame_same - gain_im[j] * flame_cross
            )
            part_im = (
                tau_re[j] * cross + tau_im[j] * same
                + gain_re[j] * flame_cross + gain_im[j] * flame_same
            )
            table = jnp.where(row8 == j, jnp.sum(part_re, axis=0, keepdims=True), table)
            table = jnp.where(
                row8 == offs + j, jnp.sum(part_im, axis=0, keepdims=True), table
            )
        column = jnp.sum(table, axis=1, keepdims=True)
        csend[target] = jnp.sum(
            jnp.where(lane == row8, column, 0.0), axis=0, keepdims=True
        )
        return carry

    lax.fori_loop(0, orders, couple, 0)
    scatter(csend, cpart, 7, 1, orders)
    cpart[me] = csend[me]
    lax.fori_loop(FIRST, orders, give, 0)
    wait_bytes(others(cpart), recv_sem.at[7])
    total = cpart[0]
    for k in range(1, orders):
        total = total + cpart[k]
    cslab[slab] = total

    def slab_copy(step):
        return pltpu.make_async_remote_copy(
            src_ref=cslab.at[slab],
            dst_ref=cslab.at[slab],
            send_sem=send_sem.at[8],
            recv_sem=recv_sem.at[8],
            device_id={"slab": lax.rem(slab + step, slabs)},
            device_id_type=MESH,
        )

    def slab_start(step, carry):
        slab_copy(step).start()
        return carry

    lax.fori_loop(1, slabs, slab_start, 0)

    istage[me] = mixed(me)
    keep = pltpu.make_async_copy(istage.at[me], arrived.at[me], local_sem.at[9])
    keep.start()
    wait_bytes(cslab.at[pl.ds(0, slabs - 1)], recv_sem.at[8])
    whole = cslab[0]
    for k in range(1, slabs):
        whole = whole + cslab[k]
    whole = whole * scale
    sums_ref[0:1, :] = whole[:, 0:offs]
    sums_ref[1:2, :] = whole[:, offs : 2 * offs]
    give_sums = pltpu.make_async_copy(sums_ref, coupling_hbm, local_sem.at[10])
    give_sums.start()
    keep.wait()
    give_sums.wait()

    wait_bytes(others(arrived), recv_sem.at[2])
    wait_bytes(others(dstage), send_sem.at[0])
    wait_bytes(others(astage), send_sem.at[1])
    wait_bytes(others(istage), send_sem.at[2])
    wait_bytes(others(csend), send_sem.at[7])
    wait_bytes(cslab.at[pl.ds(0, slabs - 1)], send_sem.at[8])

    @pl.when(has_above)
    def _():
        up_near().wait_send()
        up_rest().wait_send()

    @pl.when(has_below)
    def _():
        down_near().wait_send()
        down_rest().wait_send()

    @pl.when(relays_up)
    def _():
        up_far().wait_send()

    @pl.when(relays_down)
    def _():
        down_far().wait_send()


def write_out(arrived_hbm, sums_hbm, image_hbm, coupling_hbm, arrived, image, sem):
    layers, width = image.shape[1], image.shape[2]
    low_half = lax.broadcasted_iota(jnp.int32, (8, width), 0) < 4
    pieces = 4
    part = layers // pieces
    blocks = arrived.shape[0] // pieces

    def pull(piece):
        at = pl.ds(piece * blocks, blocks)
        return pltpu.make_async_copy(arrived_hbm.at[at], arrived.at[at], sem.at[piece])

    def push(piece):
        at = pl.ds(piece * part, part)
        return pltpu.make_async_copy(
            image.at[:, at, :], image_hbm.at[:, at, :], sem.at[pieces + piece]
        )

    sums = pltpu.make_async_copy(sums_hbm, coupling_hbm, sem.at[2 * pieces])
    for piece in range(pieces):
        pull(piece).start()
    sums.start()
    for piece in range(pieces):
        pull(piece).wait()

        def unpack(step, carry):
            tile = piece * (part // 8) + step
            at = pl.ds(pl.multiple_of(tile * 8, 8), 8)
            even = arrived[2 * tile]
            odd = arrived[2 * tile + 1]
            image[0, at, :] = jnp.where(low_half, even, pltpu.roll(odd, 4, 0))
            image[1, at, :] = jnp.where(low_half, pltpu.roll(even, 4, 0), odd)
            return carry

        lax.fori_loop(0, part // 8, unpack, 0)
        push(piece).start()
    for piece in range(pieces):
        push(piece).wait()
    sums.wait()


def solution(mesh):
    orders = mesh.shape["order"]
    slabs = mesh.shape["slab"]

    def local(
        direct, adjoint, sound, transverse, burner_temp, burner_gain, flame_cells, flame_weight, offsets
    ):
        layers, width = direct.shape[2], direct.shape[3]
        offs = offsets.shape[0]
        f32, bf16 = jnp.float32, jnp.bfloat16
        hbm = pl.BlockSpec(memory_space=pltpu.HBM)
        block = (orders, 8, width)
        arrived, sums = pl.pallas_call(
            functools.partial(
                kernel, orders, slabs, 1.0 / math.sqrt(layers * slabs * width)
            ),
            out_shape=(
                jax.ShapeDtypeStruct(block, f32),
                jax.ShapeDtypeStruct((2, offs), f32),
            ),
            in_specs=[hbm] * 9,
            out_specs=(hbm, hbm),
            scratch_shapes=[
                pltpu.VMEM((2, layers, width), f32),
                pltpu.VMEM((2, layers, width), f32),
                pltpu.VMEM((1, burner_temp.shape[0]), f32),
                pltpu.VMEM((1, burner_gain.shape[0]), f32),
                pltpu.VMEM((1, flame_cells.shape[0]), jnp.int32),
                pltpu.VMEM((1, flame_weight.shape[0]), f32),
                pltpu.SMEM((offs,), jnp.int32),
                pltpu.VMEM(block, f32),
                pltpu.VMEM(block, f32),
                pltpu.VMEM(block, f32),
                pltpu.VMEM(block, f32),
                pltpu.VMEM(block, f32),
                pltpu.VMEM(block, f32),
                pltpu.VMEM(block, f32),
                pltpu.VMEM((orders * 8, width), bf16),
                pltpu.VMEM((orders * 8, width), bf16),
                pltpu.VMEM((width, width), f32),
                pltpu.VMEM((width, width), bf16),
                pltpu.VMEM((width, width), bf16),
                pltpu.VMEM((layers + 16, width), f32),
                pltpu.VMEM((2, 2 * orders, width), f32),
                pltpu.VMEM((2, 2 * orders, width), f32),
                pltpu.VMEM((orders, width), f32),
                pltpu.VMEM((orders, 8, 128), f32),
                pltpu.VMEM((orders, 8, 128), f32),
                pltpu.VMEM((orders, 1, 128), f32),
                pltpu.VMEM((orders, 1, 128), f32),
                pltpu.VMEM((slabs, 1, 128), f32),
                pltpu.VMEM((2, offs), f32),
                pltpu.SemaphoreType.DMA((11,)),
                pltpu.SemaphoreType.DMA((12,)),
                pltpu.SemaphoreType.DMA((12,)),
            ],
            compiler_params=pltpu.CompilerParams(
                collective_id=0, has_side_effects=True, vmem_limit_bytes=58 * 2**20
            ),
        )(
            direct[0],
            adjoint[0],
            sound,
            transverse,
            burner_temp[None],
            burner_gain[None],
            flame_cells[None],
            flame_weight[None],
            offsets,
        )
        image, coupling = pl.pallas_call(
            write_out,
            out_shape=(
                jax.ShapeDtypeStruct((2, layers, width), f32),
                jax.ShapeDtypeStruct((2, offs), f32),
            ),
            in_specs=[hbm, hbm],
            out_specs=(hbm, hbm),
            scratch_shapes=[
                pltpu.VMEM(block, f32),
                pltpu.VMEM((2, layers, width), f32),
                pltpu.SemaphoreType.DMA((9,)),
            ],
            compiler_params=pltpu.CompilerParams(vmem_limit_bytes=58 * 2**20),
        )(arrived, sums)
        return image[None], coupling[None]

    in_specs = (
        P("order", None, "slab", None),
        P("order", None, "slab", None),
        P("slab", None),
        P(),
        P(),
        P(),
        P(),
        P(),
        P(),
    )
    out_specs = (P("order", None, "slab", None), P("order", None, None))
    return jax.shard_map(local, mesh=mesh, in_specs=in_specs, out_specs=out_specs, check_vma=False)
```

```python
import functools
import math

import jax
import jax.numpy as jnp
from jax import lax
from jax.experimental import pallas as pl
from jax.experimental.pallas import tpu as pltpu
from jax.sharding import PartitionSpec as P

MESH = pl.DeviceIdType.MESH
STRIDE = 11
IMAGE_STRIDE = 5
EARLY = 20
MIDDLE = 26
FIRST = 18


def kernel(
    orders,
    slabs,
    scale,
    direct_hbm,
    adjoint_hbm,
    sound_hbm,
    transverse_hbm,
    temp_hbm,
    gain_hbm,
    cells_hbm,
    weight_hbm,
    offsets_hbm,
    arrived,
    coupling_hbm,
    direct_ref,
    adjoint_ref,
    temp_ref,
    gain_ref,
    cells_ref,
    weight_ref,
    offsets_ref,
    dstage,
    astage,
    istage,
    field,
    adj,
    base,
    flamed,
    field_hi,
    field_lo,
    tmat,
    tmat_hi,
    tmat_lo,
    sound_pad,
    halo_send,
    halo_recv,
    halo_relay,
    turn_cos,
    turn_sin,
    csend,
    cpart,
    cslab,
    sums_ref,
    local_sem,
    send_sem,
    recv_sem,
):
    me = lax.axis_index("order")
    slab = lax.axis_index("slab")
    layers, width = direct_ref.shape[1], direct_ref.shape[2]
    rows = layers // orders
    last = width - 128
    offs = offsets_ref.shape[0]
    f32, bf16 = jnp.float32, jnp.bfloat16

    def order_dev(which):
        return {"order": which}

    def peer(step, stride=STRIDE):
        return lax.rem(me + lax.rem(step * stride, orders), orders)

    def fetch(source, into, sem):
        copy = pltpu.make_async_copy(source, into, local_sem.at[sem])
        copy.start()
        return copy

    pieces = 4
    part = layers // pieces
    fetch_d = [
        fetch(
            direct_hbm.at[:, pl.ds(piece * part, part), :],
            direct_ref.at[:, pl.ds(piece * part, part), :],
            11 + piece,
        )
        for piece in range(pieces)
    ]

    barrier = pltpu.get_barrier_semaphore()

    def greet_order(step, carry):
        pl.semaphore_signal(
            barrier, inc=1, device_id=order_dev(peer(step)), device_id_type=MESH
        )
        return carry

    def greet_slab(step, carry):
        pl.semaphore_signal(
            barrier,
            inc=1,
            device_id={"slab": lax.rem(slab + step, slabs)},
            device_id_type=MESH,
        )
        return carry

    has_above_slab = jnp.logical_and(me == 0, slab > 0)
    has_below_slab = jnp.logical_and(me == orders - 1, slab < slabs - 1)
    has_above = jnp.logical_or(me > 0, slab > 0)
    has_below = jnp.logical_or(me < orders - 1, slab < slabs - 1)
    above_dev = {
        "order": lax.rem(me + orders - 1, orders),
        "slab": lax.rem(slab + slabs - lax.div(orders - me, orders), slabs),
    }
    below_dev = {
        "order": lax.rem(me + 1, orders),
        "slab": lax.rem(slab + lax.div(me + 1, orders), slabs),
    }
    place_in_plane = lax.rem(me, 4)
    crosses_up = jnp.logical_and(place_in_plane == 0, has_above)
    crosses_down = jnp.logical_and(place_in_plane == 3, has_below)
    within_up = jnp.logical_and(place_in_plane != 0, has_above)
    within_down = jnp.logical_and(place_in_plane != 3, has_below)
    relays_up = jnp.logical_and(
        place_in_plane == 2, jnp.logical_or(me > 3, slab > 0)
    )
    relays_down = jnp.logical_and(
        place_in_plane == 1, jnp.logical_or(me < orders - 4, slab < slabs - 1)
    )
    far_up_dev = {
        "order": lax.rem(me + orders - 3, orders),
        "slab": lax.rem(slab + slabs - lax.div(orders + 2 - me, orders), slabs),
    }
    far_down_dev = {
        "order": lax.rem(me + 3, orders),
        "slab": lax.rem(slab + lax.div(me + 3, orders), slabs),
    }
    greet_up_dev = {"order": orders - 3, "slab": lax.rem(slab + slabs - 1, slabs)}
    greet_down_dev = {"order": 2, "slab": lax.rem(slab + 1, slabs)}
    lax.fori_loop(1, orders, greet_order, 0)
    lax.fori_loop(1, slabs, greet_slab, 0)

    @pl.when(has_above_slab)
    def _():
        pl.semaphore_signal(barrier, inc=1, device_id=above_dev, device_id_type=MESH)
        pl.semaphore_signal(
            barrier, inc=1, device_id=greet_up_dev, device_id_type=MESH
        )

    @pl.when(has_below_slab)
    def _():
        pl.semaphore_signal(barrier, inc=1, device_id=below_dev, device_id_type=MESH)
        pl.semaphore_signal(
            barrier, inc=1, device_id=greet_down_dev, device_id_type=MESH
        )

    sub = lax.broadcasted_iota(jnp.int32, (8, 128), 0)
    lane = lax.broadcasted_iota(jnp.int32, (8, 128), 1)
    sub_w = lax.broadcasted_iota(jnp.int32, (8, width), 0)

    def pack(source, stage, first, end):
        def body(tile, carry):
            at = pl.multiple_of(tile * 8, 8)
            re = source[0, pl.ds(at, 8), :]
            im = source[1, pl.ds(at, 8), :]
            stage[2 * tile] = jnp.where(sub_w < 4, re, pltpu.roll(im, 4, 0))
            stage[2 * tile + 1] = jnp.where(sub_w < 4, pltpu.roll(re, 4, 0), im)
            return carry

        lax.fori_loop(first, end, body, 0)

    fetch_c = fetch(sound_hbm, sound_pad.at[pl.ds(8, layers)], 1)
    fetch_a = fetch(adjoint_hbm, adjoint_ref, 3)
    small = [
        fetch(offsets_hbm, offsets_ref, 4),
        fetch(temp_hbm, temp_ref, 5),
        fetch(gain_hbm, gain_ref, 6),
        fetch(cells_hbm, cells_ref, 7),
        fetch(weight_hbm, weight_ref, 8),
    ]
    fetch_t = fetch(transverse_hbm, tmat, 0)
    for piece in range(pieces):
        fetch_d[piece].wait()
        pack(direct_ref, dstage, piece * part // 8, (piece + 1) * part // 8)

    near_top = jnp.logical_and(me == 2, slab > 0)
    near_bottom = jnp.logical_and(me == orders - 3, slab < slabs - 1)
    extra = has_above_slab.astype(jnp.int32) + has_below_slab.astype(jnp.int32)
    extra = extra + near_top.astype(jnp.int32) + near_bottom.astype(jnp.int32)
    pl.semaphore_wait(barrier, orders - 1 + slabs - 1 + extra)

    def scatter_copy(stage, into, sem, step):
        to = peer(step, STRIDE if sem < 2 else IMAGE_STRIDE)
        return pltpu.make_async_remote_copy(
            src_ref=stage.at[to],
            dst_ref=into.at[me],
            send_sem=send_sem.at[sem],
            recv_sem=recv_sem.at[sem],
            device_id=order_dev(to),
            device_id_type=MESH,
        )

    def scatter(stage, into, sem, first, end):
        def body(step, carry):
            scatter_copy(stage, into, sem, step).start()
            return carry

        lax.fori_loop(first, end, body, 0)

    def wait_bytes(ref, sem):
        pltpu.make_async_copy(ref, ref, sem).wait()

    def others(ref):
        return ref.at[pl.ds(0, orders - 1)]

    scatter(dstage, field, 0, 1, orders)
    field[me] = dstage[me]

    fetch_c.wait()

    def sound_up():
        return pltpu.make_async_remote_copy(
            src_ref=sound_pad.at[pl.ds(8, 8)],
            dst_ref=sound_pad.at[pl.ds(8 + layers, 8)],
            send_sem=send_sem.at[3],
            recv_sem=recv_sem.at[3],
            device_id={"slab": lax.rem(slab + slabs - 1, slabs)},
            device_id_type=MESH,
        )

    def sound_down():
        return pltpu.make_async_remote_copy(
            src_ref=sound_pad.at[pl.ds(layers, 8)],
            dst_ref=sound_pad.at[pl.ds(0, 8)],
            send_sem=send_sem.at[4],
            recv_sem=recv_sem.at[4],
            device_id={"slab": lax.rem(slab + 1, slabs)},
            device_id_type=MESH,
        )

    @pl.when(slab > 0)
    def _():
        sound_up().start()

    @pl.when(slab < slabs - 1)
    def _():
        sound_down().start()

    fetch_a.wait()
    pack(adjoint_ref, astage, 0, layers // 8)
    scatter(astage, adj, 1, 1, EARLY)
    adj[me] = astage[me]

    for copy in small:
        copy.wait()
    bin_ids = lax.broadcasted_iota(jnp.int32, (1, temp_ref.shape[1]), 1)
    tau_re, tau_im, gain_re, gain_im = [], [], [], []
    for j in range(offs):
        turns = lax.rem(offsets_ref[j] * bin_ids, orders)
        angles = 2.0 * math.pi / orders * turns.astype(f32)
        cos, sin = jnp.cos(angles), jnp.sin(angles)
        tau_re.append(jnp.sum(temp_ref[...] * cos) * (1.0 / orders))
        tau_im.append(-jnp.sum(temp_ref[...] * sin) * (1.0 / orders))
        gain_re.append(jnp.sum(gain_ref[...] * cos) * (1.0 / orders))
        gain_im.append(-jnp.sum(gain_ref[...] * sin) * (1.0 / orders))

    def turn_table(source, carry):
        angle = jnp.full((8, 128), 2.0 * math.pi / orders, f32) * source.astype(f32)
        turn_cos[source] = jnp.cos(angle)
        turn_sin[source] = jnp.where(sub < 4, -1.0, 1.0) * jnp.sin(angle)
        return carry

    lax.fori_loop(0, orders, turn_table, 0)

    first_cell = (slab * layers + me * rows) * width
    flame_step = 512
    flames = cells_ref.shape[1]
    sub_f = lax.broadcasted_iota(jnp.int32, (8, flame_step), 0)
    sub_c = lax.broadcasted_iota(jnp.int32, (width, flame_step), 0)

    def place(step, total):
        at = pl.multiple_of(step * flame_step, flame_step)
        ids = cells_ref[:, pl.ds(at, flame_step)] - first_cell
        weights = weight_ref[:, pl.ds(at, flame_step)]
        row = ids >> (width.bit_length() - 1)
        column = ids & (width - 1)
        mine = row == (sub_f & (rows - 1))
        spread = jnp.where(mine, weights, 0.0)
        hi = spread.astype(bf16)
        rest = spread - hi.astype(f32)
        mid = rest.astype(bf16)
        low = (rest - mid.astype(f32)).astype(bf16)
        pick = jnp.where(sub_c == column, 1.0, 0.0).astype(bf16)
        left = jnp.concatenate([hi.astype(f32), mid.astype(f32), low.astype(f32)], axis=0)
        part = lax.dot_general(
            left.astype(bf16), pick, (((1,), (1,)), ((), ())), preferred_element_type=f32
        )
        return total + (part[0:8] + part[8:16] + part[16:24])

    flame = lax.fori_loop(
        0, flames // flame_step, place, jnp.zeros((8, width), f32)
    )

    fetch_t.wait()

    def halves(block, carry):
        at = pl.ds(pl.multiple_of(block * 32, 32), 32)
        value = tmat[at, :]
        hi = value.astype(bf16)
        tmat_hi[at, :] = hi
        tmat_lo[at, :] = (value - hi.astype(f32)).astype(bf16)
        return carry

    lax.fori_loop(0, width // 32, halves, 0)

    @pl.when(slab < slabs - 1)
    def _():
        sound_up().wait_recv()

    @pl.when(slab > 0)
    def _():
        sound_down().wait_recv()

    @pl.when(slab < slabs - 1)
    def _():
        sound_down().wait_send()

    @pl.when(slab > 0)
    def _():
        sound_up().wait_send()

    @pl.when(slab == slabs - 1)
    def _():
        sound_pad[pl.ds(8 + layers, 8)] = jnp.zeros((8, width), f32)

    @pl.when(slab == 0)
    def _():
        sound_pad[pl.ds(0, 8)] = jnp.zeros((8, width), f32)

    tile = lax.div(me, 2)
    odd = lax.rem(me, 2) == 1
    top = sound_pad[pl.ds(pl.multiple_of(tile * 8, 8), 8), :]
    middle = sound_pad[pl.ds(pl.multiple_of(tile * 8 + 8, 8), 8), :]
    bottom = sound_pad[pl.ds(pl.multiple_of(tile * 8 + 16, 8), 8), :]
    low_half = sub_w < 4
    top_turned = pltpu.roll(top, 4, 0)
    middle_turned = pltpu.roll(middle, 4, 0)
    bottom_turned = pltpu.roll(bottom, 4, 0)
    own4 = jnp.where(odd, jnp.where(low_half, middle_turned, middle), jnp.where(low_half, middle, middle_turned))
    before = jnp.where(odd, middle, pltpu.roll(top, 4, 0))
    after = jnp.where(odd, bottom, middle_turned)
    above_row = jnp.where(low_half, pltpu.roll(before, 5, 0), pltpu.roll(before, 1, 0))
    below_row = jnp.where(low_half, pltpu.roll(after, 3, 0), pltpu.roll(after, 7, 0))
    place_in = sub_w & 3
    sound_above = jnp.where(place_in == 0, above_row, pltpu.roll(own4, 1, 0))
    sound_below = jnp.where(place_in == 3, below_row, pltpu.roll(own4, 7, 0))
    coef_below = 0.5 * (own4 + sound_below)
    coef_above = 0.5 * (own4 + sound_above)
    seam_first = 0.5 * (own4[:, 0:128] + pltpu.roll(own4[:, last:], 1, 1))
    seam_last = 0.5 * (own4[:, last:] + pltpu.roll(own4[:, 0:128], 127, 1))
    is_first = lane == 0
    is_last = lane == 127
    sign = jnp.where(sub < 4, -1.0, 1.0)
    sign_w = jnp.where(sub_w < 4, -1.0, 1.0)

    wait_bytes(others(field), recv_sem.at[0])

    def edges(group, carry):
        low = jnp.zeros((8, width), f32)
        high = jnp.zeros((8, width), f32)
        for i in range(4):
            value = field[4 * group + i]
            low = jnp.where(sub_w == 2 * i, pltpu.roll(value, (2 * i) % 8, 0), low)
            low = jnp.where(sub_w == 2 * i + 1, pltpu.roll(value, (2 * i + 5) % 8, 0), low)
            high = jnp.where(sub_w == 2 * i, pltpu.roll(value, (2 * i + 5) % 8, 0), high)
            high = jnp.where(sub_w == 2 * i + 1, pltpu.roll(value, (2 * i + 2) % 8, 0), high)
        at = pl.ds(pl.multiple_of(group * 8, 8), 8)
        halo_send[0, at, :] = low
        halo_send[1, at, :] = high
        return carry

    lax.fori_loop(0, orders // 4, edges, 0)

    near, rest = pl.ds(0, orders), pl.ds(orders, orders)

    def halo(source, into, sem, recv, to):
        return pltpu.make_async_remote_copy(
            src_ref=source,
            dst_ref=into,
            send_sem=send_sem.at[sem],
            recv_sem=recv_sem.at[recv],
            device_id=to,
            device_id_type=MESH,
        )

    def up_near():
        return halo(halo_send.at[0, near], halo_recv.at[1, near], 5, 5, above_dev)

    def up_rest():
        return halo(halo_send.at[0, rest], halo_recv.at[1, rest], 9, 9, above_dev)

    def up_relay():
        return halo(halo_send.at[0, rest], halo_relay, 9, 11, order_dev(lax.rem(me + 2, orders)))

    def up_far():
        return halo(halo_relay, halo_recv.at[1, rest], 11, 9, far_up_dev)

    def down_near():
        return halo(halo_send.at[1, near], halo_recv.at[0, near], 6, 6, below_dev)

    def down_rest():
        return halo(halo_send.at[1, rest], halo_recv.at[0, rest], 10, 10, below_dev)

    def down_relay():
        return halo(halo_send.at[1, rest], halo_relay, 10, 11, order_dev(lax.rem(me + orders - 2, orders)))

    def down_far():
        return halo(halo_relay, halo_recv.at[0, rest], 11, 10, far_down_dev)

    @pl.when(crosses_up)
    def _():
        up_relay().start()

    @pl.when(crosses_down)
    def _():
        down_relay().start()

    @pl.when(has_above)
    def _():
        up_near().start()

    @pl.when(has_below)
    def _():
        down_near().start()

    @pl.when(within_up)
    def _():
        up_rest().start()

    @pl.when(within_down)
    def _():
        down_rest().start()

    scatter(astage, adj, 1, EARLY, MIDDLE)

    def split(group, carry):
        value = field[pl.ds(4 * group, 4)].reshape(32, width)
        at = pl.ds(pl.multiple_of(group * 32, 32), 32)
        hi = value.astype(bf16)
        field_hi[at, :] = hi
        field_lo[at, :] = (value - hi.astype(f32)).astype(bf16)
        return carry

    lax.fori_loop(0, orders // 4, split, 0)

    @pl.when(relays_up)
    def _():
        up_relay().wait_recv()
        up_far().start()

    @pl.when(relays_down)
    def _():
        down_relay().wait_recv()
        down_far().start()

    scatter(astage, adj, 1, MIDDLE, orders)

    def across(block, carry):
        at = pl.ds(pl.multiple_of(block * 256, 256), 256)
        dot = functools.partial(jnp.dot, preferred_element_type=f32)
        t_hi = tmat_hi[:, at]
        t_lo = tmat_lo[:, at]
        hi = field_hi[...]
        product = dot(hi, t_lo) + dot(field_lo[...], t_hi) + dot(hi, t_hi)
        base[:, :, at] = product.reshape(orders, 8, 256)
        return carry

    lax.fori_loop(0, width // 256, across, 0)

    @pl.when(has_below)
    def _():
        up_near().wait_recv()
        up_rest().wait_recv()

    @pl.when(has_above)
    def _():
        down_near().wait_recv()
        down_rest().wait_recv()

    @pl.when(jnp.logical_not(has_below))
    def _():
        halo_recv[1] = jnp.zeros((2 * orders, width), f32)

    @pl.when(jnp.logical_not(has_above))
    def _():
        halo_recv[0] = jnp.zeros((2 * orders, width), f32)

    def helm(group, carry):
        at = pl.ds(pl.multiple_of(group * 8, 8), 8)
        upper = halo_recv[0, at, :]
        lower = halo_recv[1, at, :]
        for i in range(4):
            source = 4 * group + i
            value = field[source]
            up = jnp.where(
                sub_w == 0, pltpu.roll(upper, (8 - 2 * i) % 8, 0), pltpu.roll(value, 1, 0)
            )
            up = jnp.where(sub_w == 4, pltpu.roll(upper, (11 - 2 * i) % 8, 0), up)
            down = jnp.where(
                sub_w == 3, pltpu.roll(lower, (11 - 2 * i) % 8, 0), pltpu.roll(value, 7, 0)
            )
            down = jnp.where(sub_w == 7, pltpu.roll(lower, (14 - 2 * i) % 8, 0), down)
            axial = coef_below * (value - down) + coef_above * (value - up)
            base[source] = base[source] + axial
            flamed[source] = flame * value
            cos, sin = turn_cos[source], turn_sin[source]
            head, tail = value[:, 0:128], value[:, last:]
            tail_here = pltpu.roll(tail, 1, 1)
            head_here = pltpu.roll(head, 127, 1)
            behind = cos * tail_here - sin * pltpu.roll(tail_here, 4, 0)
            ahead = cos * head_here + sin * pltpu.roll(head_here, 4, 0)
            base[source, :, 0:128] = base[source, :, 0:128] + jnp.where(
                is_first, seam_first * (head - behind), 0.0
            )
            base[source, :, last:] = base[source, :, last:] + jnp.where(
                is_last, seam_last * (tail - ahead), 0.0
            )
        return carry

    lax.fori_loop(0, orders // 4, helm, 0)

    def mixed(target):
        plain = base[target]
        turned = jnp.zeros((8, width), f32)
        for j in range(offs):
            source = lax.rem(target - offsets_ref[j] + orders, orders)
            helm_src = base[source]
            flame_src = flamed[source]
            plain = plain + (helm_src * tau_re[j] + flame_src * gain_re[j])
            turned = turned + (helm_src * tau_im[j] + flame_src * gain_im[j])
        return plain + sign_w * pltpu.roll(turned, 4, 0)

    def give(step, carry):
        target = peer(step, IMAGE_STRIDE)
        istage[target] = mixed(target)
        scatter_copy(istage, arrived, 2, step).start()
        return carry

    lax.fori_loop(1, FIRST, give, 0)

    wait_bytes(others(adj), recv_sem.at[1])
    row8 = lax.broadcasted_iota(jnp.int32, (8, 128), 0)

    def fold(value):
        total = value[:, 0:128]
        for block in range(1, width // 128):
            total = total + value[:, block * 128 : block * 128 + 128]
        return total

    def couple(target, carry):
        mine = adj[target]
        mine_turned = sign_w * pltpu.roll(mine, 4, 0)
        table = jnp.zeros((8, 128), f32)
        for j in range(offs):
            source = lax.rem(target - offsets_ref[j] + orders, orders)
            helm_src = base[source]
            flame_src = flamed[source]
            same = fold(mine * helm_src)
            cross = fold(mine_turned * helm_src)
            flame_same = fold(mine * flame_src)
            flame_cross = fold(mine_turned * flame_src)
            part_re = (
                tau_re[j] * same - tau_im[j] * cross
                + gain_re[j] * flame_same - gain_im[j] * flame_cross
            )
            part_im = (
                tau_re[j] * cross + tau_im[j] * same
                + gain_re[j] * flame_cross + gain_im[j] * flame_same
            )
            table = jnp.where(row8 == j, jnp.sum(part_re, axis=0, keepdims=True), table)
            table = jnp.where(
                row8 == offs + j, jnp.sum(part_im, axis=0, keepdims=True), table
            )
        column = jnp.sum(table, axis=1, keepdims=True)
        csend[target] = jnp.sum(
            jnp.where(lane == row8, column, 0.0), axis=0, keepdims=True
        )
        return carry

    lax.fori_loop(0, orders, couple, 0)
    scatter(csend, cpart, 7, 1, orders)
    cpart[me] = csend[me]
    lax.fori_loop(FIRST, orders, give, 0)
    wait_bytes(others(cpart), recv_sem.at[7])
    total = cpart[0]
    for k in range(1, orders):
        total = total + cpart[k]
    cslab[slab] = total

    def slab_copy(step):
        return pltpu.make_async_remote_copy(
            src_ref=cslab.at[slab],
            dst_ref=cslab.at[slab],
            send_sem=send_sem.at[8],
            recv_sem=recv_sem.at[8],
            device_id={"slab": lax.rem(slab + step, slabs)},
            device_id_type=MESH,
        )

    def slab_start(step, carry):
        slab_copy(step).start()
        return carry

    lax.fori_loop(1, slabs, slab_start, 0)

    istage[me] = mixed(me)
    keep = pltpu.make_async_copy(istage.at[me], arrived.at[me], local_sem.at[9])
    keep.start()
    wait_bytes(cslab.at[pl.ds(0, slabs - 1)], recv_sem.at[8])
    whole = cslab[0]
    for k in range(1, slabs):
        whole = whole + cslab[k]
    whole = whole * scale
    sums_ref[0:1, :] = whole[:, 0:offs]
    sums_ref[1:2, :] = whole[:, offs : 2 * offs]
    give_sums = pltpu.make_async_copy(sums_ref, coupling_hbm, local_sem.at[10])
    give_sums.start()
    keep.wait()
    give_sums.wait()

    wait_bytes(others(arrived), recv_sem.at[2])
    wait_bytes(others(dstage), send_sem.at[0])
    wait_bytes(others(astage), send_sem.at[1])
    wait_bytes(others(istage), send_sem.at[2])
    wait_bytes(others(csend), send_sem.at[7])
    wait_bytes(cslab.at[pl.ds(0, slabs - 1)], send_sem.at[8])

    @pl.when(has_above)
    def _():
        up_near().wait_send()
        up_rest().wait_send()

    @pl.when(has_below)
    def _():
        down_near().wait_send()
        down_rest().wait_send()

    @pl.when(relays_up)
    def _():
        up_far().wait_send()

    @pl.when(relays_down)
    def _():
        down_far().wait_send()


def write_out(arrived_hbm, sums_hbm, image_hbm, coupling_hbm, arrived, image, sem):
    layers, width = image.shape[1], image.shape[2]
    low_half = lax.broadcasted_iota(jnp.int32, (8, width), 0) < 4
    pieces = 4
    part = layers // pieces
    blocks = arrived.shape[0] // pieces

    def pull(piece):
        at = pl.ds(piece * blocks, blocks)
        return pltpu.make_async_copy(arrived_hbm.at[at], arrived.at[at], sem.at[piece])

    def push(piece):
        at = pl.ds(piece * part, part)
        return pltpu.make_async_copy(
            image.at[:, at, :], image_hbm.at[:, at, :], sem.at[pieces + piece]
        )

    sums = pltpu.make_async_copy(sums_hbm, coupling_hbm, sem.at[2 * pieces])
    for piece in range(pieces):
        pull(piece).start()
    sums.start()
    for piece in range(pieces):
        pull(piece).wait()

        def unpack(step, carry):
            tile = piece * (part // 8) + step
            at = pl.ds(pl.multiple_of(tile * 8, 8), 8)
            even = arrived[2 * tile]
            odd = arrived[2 * tile + 1]
            image[0, at, :] = jnp.where(low_half, even, pltpu.roll(odd, 4, 0))
            image[1, at, :] = jnp.where(low_half, pltpu.roll(even, 4, 0), odd)
            return carry

        lax.fori_loop(0, part // 8, unpack, 0)
        push(piece).start()
    for piece in range(pieces):
        push(piece).wait()
    sums.wait()


def solution(mesh):
    orders = mesh.shape["order"]
    slabs = mesh.shape["slab"]

    def local(
        direct, adjoint, sound, transverse, burner_temp, burner_gain, flame_cells, flame_weight, offsets
    ):
        layers, width = direct.shape[2], direct.shape[3]
        offs = offsets.shape[0]
        f32, bf16 = jnp.float32, jnp.bfloat16
        hbm = pl.BlockSpec(memory_space=pltpu.HBM)
        block = (orders, 8, width)
        arrived, sums = pl.pallas_call(
            functools.partial(
                kernel, orders, slabs, 1.0 / math.sqrt(layers * slabs * width)
            ),
            out_shape=(
                jax.ShapeDtypeStruct(block, f32),
                jax.ShapeDtypeStruct((2, offs), f32),
            ),
            in_specs=[hbm] * 9,
            out_specs=(hbm, hbm),
            scratch_shapes=[
                pltpu.VMEM((2, layers, width), f32),
                pltpu.VMEM((2, layers, width), f32),
                pltpu.VMEM((1, burner_temp.shape[0]), f32),
                pltpu.VMEM((1, burner_gain.shape[0]), f32),
                pltpu.VMEM((1, flame_cells.shape[0]), jnp.int32),
                pltpu.VMEM((1, flame_weight.shape[0]), f32),
                pltpu.SMEM((offs,), jnp.int32),
                pltpu.VMEM(block, f32),
                pltpu.VMEM(block, f32),
                pltpu.VMEM(block, f32),
                pltpu.VMEM(block, f32),
                pltpu.VMEM(block, f32),
                pltpu.VMEM(block, f32),
                pltpu.VMEM(block, f32),
                pltpu.VMEM((orders * 8, width), bf16),
                pltpu.VMEM((orders * 8, width), bf16),
                pltpu.VMEM((width, width), f32),
                pltpu.VMEM((width, width), bf16),
                pltpu.VMEM((width, width), bf16),
                pltpu.VMEM((layers + 16, width), f32),
                pltpu.VMEM((2, 2 * orders, width), f32),
                pltpu.VMEM((2, 2 * orders, width), f32),
                pltpu.VMEM((orders, width), f32),
                pltpu.VMEM((orders, 8, 128), f32),
                pltpu.VMEM((orders, 8, 128), f32),
                pltpu.VMEM((orders, 1, 128), f32),
                pltpu.VMEM((orders, 1, 128), f32),
                pltpu.VMEM((slabs, 1, 128), f32),
                pltpu.VMEM((2, offs), f32),
                pltpu.SemaphoreType.DMA((15,)),
                pltpu.SemaphoreType.DMA((12,)),
                pltpu.SemaphoreType.DMA((12,)),
            ],
            compiler_params=pltpu.CompilerParams(
                collective_id=0, has_side_effects=True, vmem_limit_bytes=58 * 2**20
            ),
        )(
            direct[0],
            adjoint[0],
            sound,
            transverse,
            burner_temp[None],
            burner_gain[None],
            flame_cells[None],
            flame_weight[None],
            offsets,
        )
        image, coupling = pl.pallas_call(
            write_out,
            out_shape=(
                jax.ShapeDtypeStruct((2, layers, width), f32),
                jax.ShapeDtypeStruct((2, offs), f32),
            ),
            in_specs=[hbm, hbm],
            out_specs=(hbm, hbm),
            scratch_shapes=[
                pltpu.VMEM(block, f32),
                pltpu.VMEM((2, layers, width), f32),
                pltpu.SemaphoreType.DMA((9,)),
            ],
            compiler_params=pltpu.CompilerParams(vmem_limit_bytes=58 * 2**20),
        )(arrived, sums)
        return image[None], coupling[None]

    in_specs = (
        P("order", None, "slab", None),
        P("order", None, "slab", None),
        P("slab", None),
        P(),
        P(),
        P(),
        P(),
        P(),
        P(),
    )
    out_specs = (P("order", None, "slab", None), P("order", None, None))
    return jax.shard_map(local, mesh=mesh, in_specs=in_specs, out_specs=out_specs, check_vma=False)
```
